256 devices in a mesh: resp: 32 (over x, z), kvh: 8 (over y, core).
Axes of the slice: x: 4, y: 4, z: 8, core: 2. Of those that a mesh axis runs over, the one named last changes fastest.
Arguments:
- query: bfloat16 [32, 256, 8192], P('resp', None, 'kvh'), may hold values from -8 to 8
- output_gradient: bfloat16 [32, 256, 8192], P('resp', None, 'kvh'), may hold values from -6 to 6
- prompt_key_pool: bfloat16 [128, 128, 1024], P('resp', 'kvh'), may hold values from -8 to 8
- prompt_value_pool: bfloat16 [128, 128, 1024], P('resp', 'kvh'), may hold values from -6 to 6
- block_tables: int32 [32, 16], replicated, may hold values from 0 to 127, as said below
- lengths: int32 [32], P('resp'), may hold values from 32 to 256, as said below
Outputs:
- grad_query: bfloat16 [32, 256, 8192], P('resp', None, 'kvh')
- grad_key: float32 [128, 128, 1024], P('resp', 'kvh')
- grad_value: float32 [128, 128, 1024], P('resp', 'kvh')
The draws below stay inside these ranges and needn't reach their ends.
Inputs may be any that keep to these rules, and one draw needn't show every extreme that they name: `block_tables`: response r reads the pages of prompt r // 16: all 16 responses of a prompt have the same table. A table names 16 distinct pages; pool page p is owned by index p // 4 of resp, and the pages of a table lie on 8 owners with exactly 2 on each. `lengths`: some response has all 256 tokens live.
All inputs are finite; a program needn't handle non-finite values.
Results may differ from the reference program's by a relative error of at most 0.011.
Values may be sent and summed in bfloat16 or wider, within the bound.
A program may use at most 128 MiB of HBM per device.

```python
import jax
import jax.numpy as jnp
from jax import lax

QUERY_HEADS = 64
KEY_VALUE_HEADS = 8
HEAD_WIDTH = 128
RESPONSE_TOKENS = 256
PAGE_TOKENS = 128
PROMPT_PAGES = 16
PAGES_DEV = 4
RESPONSES = 32
SHARE = 16
POOL_PAGES = 128


def draw_query(key, part):
    key = jax.random.fold_in(key, 21)
    array_shape = (RESPONSES, RESPONSE_TOKENS, QUERY_HEADS * HEAD_WIDTH)
    base = jnp.clip(jax.random.normal(key, array_shape, jnp.float32), -8.0, 8.0)
    return base.astype(jnp.bfloat16)


def draw_prompt_key_pool(key, part):
    key = jax.random.fold_in(key, 22)
    array_shape = (POOL_PAGES, PAGE_TOKENS, KEY_VALUE_HEADS * HEAD_WIDTH)
    base = jnp.clip(jax.random.normal(key, array_shape, jnp.float32), -8.0, 8.0)
    return base.astype(jnp.bfloat16)


def draw_block_tables(key, part):
    key = jax.random.fold_in(key, 11)
    prompts = RESPONSES // SHARE
    first, second, third = jax.random.split(key, 3)
    owner_perm = jax.vmap(lambda k: jax.random.permutation(k, RESPONSES))(jax.random.split(first, prompts))
    owners = owner_perm[:, jnp.arange(PROMPT_PAGES) // 2]
    local_perm = jax.vmap(lambda k: jax.random.permutation(k, PAGES_DEV))(jax.random.split(second, prompts * (PROMPT_PAGES // 2)))
    local_page = local_perm[:, :2].reshape(prompts, PROMPT_PAGES)
    slots = owners * PAGES_DEV + local_page
    order = jax.vmap(lambda k: jax.random.permutation(k, PROMPT_PAGES))(jax.random.split(third, prompts))
    tables = jnp.take_along_axis(slots, order, axis=1)
    return jnp.repeat(tables, SHARE, axis=0).astype(jnp.int32)


def draw_lengths(key, part):
    key = jax.random.fold_in(key, 12)
    first, second = jax.random.split(key)
    drawn = jax.random.randint(first, (RESPONSES,), max(RESPONSE_TOKENS // 8, 1), RESPONSE_TOKENS + 1)
    picked = jax.random.randint(second, (), 0, RESPONSES)
    return drawn.at[picked].set(RESPONSE_TOKENS).astype(jnp.int32)


def levels(own_key, dims, cuts, smallest, top_value):
    loudness = 1.0
    for position, parts in cuts:
        draws = jax.random.uniform(jax.random.fold_in(jax.random.fold_in(own_key, 6), position), (parts,), jnp.float32, smallest / len(cuts), top_value / len(cuts))
        loudness = loudness * jnp.repeat(jnp.exp(draws), dims[position] // parts).reshape((-1,) + (1,) * (len(dims) - 1 - position))
    return loudness


def normal_values(own_key, extent, spread, limit, cuts=(), kind=jnp.bfloat16):
    values = jax.random.normal(own_key, extent, jnp.float32) * spread
    if len(cuts) > 0:
        values = levels(own_key, extent, cuts, -0.22, 0.18) * values
    return jnp.clip(values, min=-limit, max=limit).astype(kind)


def setup_inputs(seed: int = 0) -> dict:
    streams_of = jax.random.split(jax.random.key(seed), 7)
    query = draw_query(jax.random.fold_in(streams_of[6], 71), 0)
    output_gradient = normal_values(streams_of[1], (RESPONSES, RESPONSE_TOKENS, QUERY_HEADS * HEAD_WIDTH), 1.0, 6.0, ((0, 32), (2, 8)))
    prompt_key_pool = draw_prompt_key_pool(jax.random.fold_in(streams_of[6], 71), 0)
    prompt_value_pool = normal_values(streams_of[3], (POOL_PAGES, PAGE_TOKENS, KEY_VALUE_HEADS * HEAD_WIDTH), 1.0, 6.0, ((0, 32), (1, 8)))
    block_tables = draw_block_tables(jax.random.fold_in(streams_of[6], 71), 0)
    lengths = draw_lengths(jax.random.fold_in(streams_of[6], 71), 0)
    return dict(query=query, output_gradient=output_gradient, prompt_key_pool=prompt_key_pool, prompt_value_pool=prompt_value_pool, block_tables=block_tables, lengths=lengths)


def reference(query, output_gradient, prompt_key_pool, prompt_value_pool, block_tables, lengths):
    score_scale = HEAD_WIDTH ** -0.5
    group_width = QUERY_HEADS // KEY_VALUE_HEADS
    key_row_block = PROMPT_PAGES * PAGE_TOKENS

    def per_response(totals, response_index):
        key_gradient, value_gradient = totals
        response_table = block_tables[response_index]
        paged_keys = prompt_key_pool[response_table].reshape(key_row_block, KEY_VALUE_HEADS, HEAD_WIDTH).astype(jnp.float32)
        paged_values = prompt_value_pool[response_table].reshape(key_row_block, KEY_VALUE_HEADS, HEAD_WIDTH).astype(jnp.float32)
        query_rows = query[response_index].reshape(RESPONSE_TOKENS, KEY_VALUE_HEADS, group_width, HEAD_WIDTH).astype(jnp.float32)
        upstream_gradient = output_gradient[response_index].reshape(RESPONSE_TOKENS, KEY_VALUE_HEADS, group_width, HEAD_WIDTH).astype(jnp.float32)
        live_rows = (jnp.arange(RESPONSE_TOKENS) < lengths[response_index])[:, None, None, None]
        scores = jnp.einsum("thgd,khd->thgk", query_rows, paged_keys) * score_scale
        attention = jax.nn.softmax(scores, axis=-1)
        grad_attn = jnp.einsum("thgd,khd->thgk", upstream_gradient, paged_values)
        delta_rows = jnp.sum(attention * grad_attn, axis=-1, keepdims=True)
        grad_scores = attention * (grad_attn - delta_rows)
        attention_b = lax.optimization_barrier(jnp.where(live_rows, attention, 0.0).astype(jnp.bfloat16)).astype(jnp.float32)
        scores_b = lax.optimization_barrier(jnp.where(live_rows, grad_scores, 0.0).astype(jnp.bfloat16)).astype(jnp.float32)
        grad_queries = (jnp.einsum("thgk,khd->thgd", scores_b, paged_keys) * score_scale).astype(jnp.bfloat16)
        key_portion = jnp.einsum("thgk,thgd->khd", scores_b, query_rows) * score_scale
        value_portion = jnp.einsum("thgk,thgd->khd", attention_b, upstream_gradient)
        key_gradient = key_gradient.at[response_table].add(key_portion.reshape(PROMPT_PAGES, PAGE_TOKENS, KEY_VALUE_HEADS * HEAD_WIDTH))
        value_gradient = value_gradient.at[response_table].add(value_portion.reshape(PROMPT_PAGES, PAGE_TOKENS, KEY_VALUE_HEADS * HEAD_WIDTH))
        return (key_gradient, value_gradient), grad_queries.reshape(RESPONSE_TOKENS, QUERY_HEADS * HEAD_WIDTH)

    zero_filled = jnp.zeros((POOL_PAGES, PAGE_TOKENS, KEY_VALUE_HEADS * HEAD_WIDTH), jnp.float32)
    (grad_key, grad_value), grad_query = lax.scan(per_response, (zero_filled, zero_filled), jnp.arange(RESPONSES))
    return grad_query, grad_key, grad_value
```

```python
import functools

import jax
import jax.numpy as jnp
from jax import lax
from jax.experimental import pallas as pl
from jax.experimental.pallas import tpu as pltpu
from jax.sharding import PartitionSpec as P

QUERY_HEADS = 64
KEY_VALUE_HEADS = 8
HEAD_WIDTH = 128
PAGES_DEV = 4
SLOTS = 2
ROWS = 16
MESH = pl.DeviceIdType.MESH
LOG2E = 1.4426950408889634


def place():
    rings = lax.axis_size("kvh")
    own = lax.axis_index("resp")
    head = lax.axis_index("kvh")
    return own, head, own // rings, lax.rem(own, rings), rings


def mod(value, size):
    return lax.rem(value + 2 * size, size)


def local_slots(tables, prompt, own, share, pages):
    first, second, count = jnp.int32(-1), jnp.int32(-1), jnp.int32(0)
    for j in range(pages):
        page = tables[prompt * share, j]
        hit = (page // PAGES_DEV) == own
        local = lax.rem(page, PAGES_DEV)
        first = jnp.where(hit & (count == 0), local, first)
        second = jnp.where(hit & (count == 1), local, second)
        count = count + hit.astype(jnp.int32)
    return first, second


def prompt_owners(tables, prompt, share, pages):
    held = [tables[prompt * share, j] // PAGES_DEV for j in range(pages)]
    ranks = []
    for j in range(pages):
        below = jnp.int32(0)
        for i in range(pages):
            if i != j:
                below = below + (held[i] < held[j]).astype(jnp.int32)
        ranks.append(below // SLOTS)
    owners = []
    for n in range(pages // SLOTS):
        owner = jnp.int32(0)
        for j in range(pages):
            owner = jnp.where(ranks[j] == n, held[j], owner)
        owners.append(owner)
    return owners


def spread_peers(own_x, own_z, head, rings, x_count):
    def target(i):
        dx, dh = i // rings, lax.rem(i, rings)
        x = lax.rem(own_x + dx, x_count)
        h = lax.rem(head + dh, rings)
        z = mod(own_z - dh + 1, rings)
        return x, h, z

    def origin(i):
        dx, dk = i // rings, lax.rem(i, rings)
        x = lax.rem(own_x + dx, x_count)
        k = lax.rem(head + dk, rings)
        z = mod(own_z - dk - 1, rings)
        return x, k, z

    return target, origin


def ring_peers(own_x, own_z, rings):
    right = own_x * rings + lax.rem(own_z + 1, rings)
    left = own_x * rings + mod(own_z - 1, rings)
    buddy = (own_x + 1 - 2 * lax.rem(own_x, 2)) * rings + own_z
    return right, left, buddy


def gather_kernel(share, pages, tables, key_pool, value_pool, out, stage, recv,
                  spread_send, spread_recv, send_sem, recv_sem):
    own, head, own_x, own_z, rings = place()
    x_count = lax.axis_size("resp") // rings
    target, origin = spread_peers(own_x, own_z, head, rings, x_count)
    right, left, buddy = ring_peers(own_x, own_z, rings)
    messages = x_count * rings

    barrier = pltpu.get_barrier_semaphore()

    def greet(i, carry):
        x, k, z = origin(i)
        pl.semaphore_signal(barrier, inc=1, device_id=(x * rings + z, k), device_id_type=MESH)
        return carry

    lax.fori_loop(0, messages, greet, 0)
    for peer in (right, left, buddy):
        pl.semaphore_signal(barrier, inc=1, device_id=(peer, head), device_id_type=MESH)

    for prompt in range(x_count // 2):
        picked = local_slots(tables, prompt, own, share, pages)
        for slot in range(SLOTS):
            page = jnp.maximum(picked[slot], 0)
            for h in range(rings):
                columns = slice(h * HEAD_WIDTH, (h + 1) * HEAD_WIDTH)
                stage[prompt * SLOTS + slot, h, :ROWS, :] = key_pool[page, :, columns]
                stage[prompt * SLOTS + slot, h, ROWS:, :] = value_pool[page, :, columns]

    pl.semaphore_wait(barrier, messages + 3)

    def send(i, carry):
        x, h, z = target(i)
        pltpu.make_async_remote_copy(
            src_ref=stage.at[x, h], dst_ref=recv.at[own], send_sem=spread_send, recv_sem=spread_recv,
            device_id=(x * rings + z, h), device_id_type=MESH,
        ).start()
        return carry

    lax.fori_loop(0, messages, send, 0)
    owners = prompt_owners(tables, own_x // 2, share, pages)
    pltpu.make_async_copy(recv, recv, spread_recv).wait()

    side = lax.rem(own_x, 2)
    mine = side * rings + own_z
    for n, owner in enumerate(owners):
        piece = recv[owner]
        out[mine, 0, n * ROWS:(n + 1) * ROWS, :] = piece[:ROWS]
        out[mine, 1, n * ROWS:(n + 1) * ROWS, :] = piece[ROWS:]

    copies = []
    slot_of = {}

    def push(name, chunk, part, peer):
        slot = slot_of.setdefault(name, len(slot_of))
        copy = pltpu.make_async_remote_copy(
            src_ref=out.at[chunk, part], dst_ref=out.at[chunk, part],
            send_sem=send_sem.at[slot], recv_sem=recv_sem.at[slot],
            device_id=(peer, head), device_id_type=MESH,
        )
        copy.start()
        copies.append(copy)
        return copy

    other = (1 - side) * rings
    same = side * rings
    hops = {1: rings // 2, -1: rings // 2 - 1}
    peers = {1: right, -1: left}
    moving = {}
    moving["x", 1] = push(("x", 1), mine, 1, buddy)
    for way in (1, -1):
        for part in (0, 1):
            moving["z", way, 0, part, 0] = push(("z", way, 0, part, 0), mine, part, peers[way])
    moving["x", 0, 0] = push(("x", 0, 0), mine, 0, buddy)
    moving["x", 1].wait_recv()
    for way in (1, -1):
        moving["z", way, 0, 1, 1] = push(("z", way, 0, 1, 1), other + own_z, 1, peers[way])
    for step in range(1, rings // 2 + 1):
        for part, flip in ((0, 0), (1, 0), (1, 1)):
            for way in (1, -1):
                if step > hops[way]:
                    continue
                moving["z", way, step - 1, part, flip].wait_recv()
                chunk = (other if flip else same) + mod(own_z - way * step, rings)
                if step < hops[way]:
                    name = ("z", way, step, part, flip)
                    moving[name] = push(name, chunk, part, peers[way])
                if part == 0:
                    name = ("x", 0, way * step)
                    moving[name] = push(name, chunk, part, buddy)
    for name, copy in moving.items():
        if name[0] == "x" and name[1] == 0:
            copy.wait_recv()
    for copy in copies:
        copy.wait_send()
    pltpu.make_async_copy(stage, stage, spread_send).wait()


def gather_copies(rings):
    return 1 + rings + 3 * (rings - 1)


def gathered(tables, key_pool, value_pool, share, pages):
    rings = lax.axis_size("kvh")
    devices = lax.axis_size("resp")
    x_count = devices // rings
    rows = rings * ROWS
    return pl.pallas_call(
        functools.partial(gather_kernel, share, pages),
        out_shape=jax.ShapeDtypeStruct((SLOTS * rings, 2, rows, HEAD_WIDTH), jnp.bfloat16),
        in_specs=[
            pl.BlockSpec(memory_space=pltpu.SMEM),
            pl.BlockSpec(memory_space=pltpu.VMEM),
            pl.BlockSpec(memory_space=pltpu.VMEM),
        ],
        out_specs=pl.BlockSpec(memory_space=pltpu.VMEM),
        scratch_shapes=[
            pltpu.VMEM((x_count, rings, 2 * ROWS, HEAD_WIDTH), jnp.bfloat16),
            pltpu.VMEM((devices, 2 * ROWS, HEAD_WIDTH), jnp.bfloat16),
            pltpu.SemaphoreType.DMA,
            pltpu.SemaphoreType.DMA,
            pltpu.SemaphoreType.DMA((gather_copies(rings),)),
            pltpu.SemaphoreType.DMA((gather_copies(rings),)),
        ],
        compiler_params=pltpu.CompilerParams(
            collective_id=0, has_side_effects=True, vmem_limit_bytes=16 * 2**20
        ),
    )(tables, key_pool, value_pool)


def attention_kernel(chunk_rows, lengths, query, upstream, pages, grad_query, grad_pages,
                     keys_t, score, slope, soft):
    group = pl.program_id(0)
    chunks = pages.shape[0]
    tokens = query.shape[0]
    scale = HEAD_WIDTH ** -0.5
    rows_t = (((1,), (1,)), ((), ()))

    @pl.when(group == 0)
    def _():
        def turn(c, carry):
            keys_t[c] = pages[c, 0].T
            grad_pages[c] = jnp.zeros_like(grad_pages[c])
            return carry
        lax.fori_loop(0, chunks, turn, 0)

    query_t = query[...].T
    upstream_t = upstream[...].T

    def scores(c, top):
        part = jnp.dot(pages[c, 0], query_t, preferred_element_type=jnp.float32) * (scale * LOG2E)
        score[c] = part
        slope[c] = jnp.dot(pages[c, 1], upstream_t, preferred_element_type=jnp.float32)
        return jnp.maximum(top, jnp.max(part.reshape(-1, 8, tokens), axis=0))

    top = lax.fori_loop(0, chunks, scores, jnp.full((8, tokens), -jnp.inf, jnp.float32))
    top = jnp.max(top, axis=0, keepdims=True)

    def weights(c, carry):
        total, delta = carry
        part = jnp.exp2(score[c] - top)
        score[c] = part
        soft[c] = part.astype(jnp.bfloat16)
        total = total + jnp.sum(part.reshape(-1, 8, tokens), axis=0)
        delta = delta + jnp.sum((part * slope[c]).reshape(-1, 8, tokens), axis=0)
        return total, delta

    zero = jnp.zeros((8, tokens), jnp.float32)
    total, delta = lax.fori_loop(0, chunks, weights, (zero, zero))
    inverse = 1.0 / jnp.sum(total, axis=0, keepdims=True)
    delta = jnp.sum(delta, axis=0, keepdims=True) * inverse
    live = lax.broadcasted_iota(jnp.int32, (1, tokens), 1) < lengths[0]
    inverse = jnp.where(live, inverse, 0.0)
    query_s = (query_t.astype(jnp.float32) * (inverse * scale)).astype(jnp.bfloat16)
    upstream_s = (upstream_t.astype(jnp.float32) * inverse).astype(jnp.bfloat16)

    def gradients(c, total):
        slopes = (score[c] * (slope[c] - delta)).astype(jnp.bfloat16)
        grad_pages[c, 0] += lax.dot_general(slopes, query_s, rows_t, preferred_element_type=jnp.float32)
        grad_pages[c, 1] += lax.dot_general(soft[c], upstream_s, rows_t, preferred_element_type=jnp.float32)
        return total + jnp.dot(keys_t[c], slopes, preferred_element_type=jnp.float32)

    total = lax.fori_loop(0, chunks, gradients, jnp.zeros((HEAD_WIDTH, tokens), jnp.float32))
    grad_query[...] = (total * (inverse * scale)).T.astype(jnp.bfloat16)


def attention_gradients(lengths, query, upstream, pages):
    tokens, width = query.shape
    groups = width // HEAD_WIDTH
    chunks, _, rows, _ = pages.shape
    block = pl.BlockSpec((tokens, HEAD_WIDTH), lambda g: (0, g))
    whole = pl.BlockSpec(pages.shape, lambda g: (0, 0, 0, 0))
    return pl.pallas_call(
        functools.partial(attention_kernel, rows),
        grid=(groups,),
        out_shape=(
            jax.ShapeDtypeStruct(query.shape, jnp.bfloat16),
            jax.ShapeDtypeStruct(pages.shape, jnp.float32),
        ),
        in_specs=[pl.BlockSpec(memory_space=pltpu.SMEM), block, block, whole],
        out_specs=(block, whole),
        scratch_shapes=[
            pltpu.VMEM((chunks, HEAD_WIDTH, rows), jnp.bfloat16),
            pltpu.VMEM((chunks, rows, tokens), jnp.float32),
            pltpu.VMEM((chunks, rows, tokens), jnp.float32),
            pltpu.VMEM((chunks, rows, tokens), jnp.bfloat16),
        ],
        compiler_params=pltpu.CompilerParams(vmem_limit_bytes=32 * 2**20),
    )(lengths, query, upstream, pages)


def scatter_kernel(share, pages, tables, grads, grad_key, grad_value,
                   x_out, x_in, z_out, z_in, total, packed, stage, recv,
                   x_send, x_recv, z_send, z_recv, back_send, back_recv):
    own, head, own_x, own_z, rings = place()
    x_count = lax.axis_size("resp") // rings
    target, origin = spread_peers(own_x, own_z, head, rings, x_count)
    right, left, buddy = ring_peers(own_x, own_z, rings)
    messages = x_count * rings

    barrier = pltpu.get_barrier_semaphore()

    def greet(i, carry):
        x, h, z = target(i)
        pl.semaphore_signal(barrier, inc=1, device_id=(x * rings + z, h), device_id_type=MESH)
        return carry

    lax.fori_loop(0, messages, greet, 0)
    for peer in (right, left, buddy):
        pl.semaphore_signal(barrier, inc=1, device_id=(peer, head), device_id_type=MESH)

    side = lax.rem(own_x, 2)
    same = side * rings
    other = (1 - side) * rings
    hops = {1: rings // 2, -1: rings // 2 - 1}
    peers = {1: right, -1: left}
    copies = []
    x_moving, z_moving = {}, {}
    order = []
    for d in range(rings // 2, 0, -1):
        order += [d, -d] if d < rings // 2 else [d]
    order.append(0)
    for n, d in enumerate(order):
        x_out[n] = grads[other + mod(own_z + d, rings), 0].astype(jnp.bfloat16)
    pl.semaphore_wait(barrier, messages + 3)

    def x_push(n):
        copy = pltpu.make_async_remote_copy(
            src_ref=x_out.at[n], dst_ref=x_in.at[n], send_sem=x_send.at[n], recv_sem=x_recv.at[n],
            device_id=(buddy, head), device_id_type=MESH,
        )
        copy.start()
        copies.append(copy)
        x_moving[n] = copy

    def z_push(way, step, item, value):
        n = (way == -1) * 3 * hops[1] + step * 3 + item
        z_out[n] = value.astype(jnp.bfloat16)
        copy = pltpu.make_async_remote_copy(
            src_ref=z_out.at[n], dst_ref=z_in.at[n], send_sem=z_send.at[n], recv_sem=z_recv.at[n],
            device_id=(peers[way], head), device_id_type=MESH,
        )
        copy.start()
        copies.append(copy)
        z_moving[way, step, item] = (copy, n)

    def z_arrived(way, step, item):
        copy, n = z_moving[way, step, item]
        copy.wait_recv()
        return z_in[n].astype(jnp.float32)

    def own_term(item, d):
        spot = mod(own_z + d, rings)
        if item == 0:
            n = order.index(d)
            x_moving[n].wait_recv()
            return grads[same + spot, 0] + x_in[n].astype(jnp.float32)
        return grads[(same if item == 1 else other) + spot, 1]

    for n in range(rings):
        x_push(n)
    for step in range(rings // 2):
        for item in (1, 2, 0):
            for way in (1, -1):
                if step >= hops[way]:
                    continue
                d = way * (hops[way] - step)
                value = own_term(item, d)
                if step > 0:
                    value = value + z_arrived(way, step - 1, item)
                z_push(way, step, item, value)

    def finish(item):
        value = own_term(item, 0)
        for way in (1, -1):
            if hops[way]:
                value = value + z_arrived(way, hops[way] - 1, item)
        return value

    x_out[rings] = finish(2).astype(jnp.bfloat16)
    x_push(rings)
    total[0] = finish(0)
    value_total = finish(1)
    x_moving[rings].wait_recv()
    total[1] = value_total + x_in[rings].astype(jnp.float32)

    for n in range(rings):
        packed[n, :ROWS, :] = total[0, n * ROWS:(n + 1) * ROWS, :].astype(jnp.bfloat16)
        packed[n, ROWS:, :] = total[1, n * ROWS:(n + 1) * ROWS, :].astype(jnp.bfloat16)
    owners = prompt_owners(tables, own_x // 2, share, pages)
    for device in range(x_count * rings):
        rank = jnp.int32(0)
        for n, owner in enumerate(owners):
            rank = jnp.where(owner == device, n, rank)
        stage[device] = packed[rank]

    def send(i, carry):
        x, k, z = origin(i)
        pltpu.make_async_remote_copy(
            src_ref=stage.at[x * rings + z], dst_ref=recv.at[own_x, head],
            send_sem=back_send, recv_sem=back_recv,
            device_id=(x * rings + z, k), device_id_type=MESH,
        ).start()
        return carry

    lax.fori_loop(0, messages, send, 0)
    picked = []
    for prompt in range(x_count // 2):
        picked += local_slots(tables, prompt, own, share, pages)
    pltpu.make_async_copy(recv, recv, back_recv).wait()
    for page in range(PAGES_DEV):
        takes = [(slot == page).astype(jnp.float32) for slot in picked]
        for h in range(rings):
            columns = slice(h * HEAD_WIDTH, (h + 1) * HEAD_WIDTH)
            value = jnp.zeros((2 * ROWS, HEAD_WIDTH), jnp.float32)
            for n, take in enumerate(takes):
                value = value + recv[n, h].astype(jnp.float32) * take
            grad_key[page, :, columns] = value[:ROWS]
            grad_value[page, :, columns] = value[ROWS:]
    for copy in copies:
        copy.wait_send()
    pltpu.make_async_copy(stage, stage, back_send).wait()


def scattered(tables, grads, share, pages):
    rings = lax.axis_size("kvh")
    devices = lax.axis_size("resp")
    x_count = devices // rings
    rows = rings * ROWS
    z_copies = 3 * (rings - 1)
    block = pltpu.VMEM((rows, HEAD_WIDTH), jnp.bfloat16)
    out = jax.ShapeDtypeStruct((PAGES_DEV, ROWS, rings * HEAD_WIDTH), jnp.float32)
    return pl.pallas_call(
        functools.partial(scatter_kernel, share, pages),
        out_shape=(out, out),
        in_specs=[pl.BlockSpec(memory_space=pltpu.SMEM), pl.BlockSpec(memory_space=pltpu.VMEM)],
        out_specs=(pl.BlockSpec(memory_space=pltpu.VMEM),) * 2,
        scratch_shapes=[
            pltpu.VMEM((rings + 1, rows, HEAD_WIDTH), jnp.bfloat16),
            pltpu.VMEM((rings + 1, rows, HEAD_WIDTH), jnp.bfloat16),
            pltpu.VMEM((z_copies, rows, HEAD_WIDTH), jnp.bfloat16),
            pltpu.VMEM((z_copies, rows, HEAD_WIDTH), jnp.bfloat16),
            pltpu.VMEM((2, rows, HEAD_WIDTH), jnp.float32),
            pltpu.VMEM((rings, 2 * ROWS, HEAD_WIDTH), jnp.bfloat16),
            pltpu.VMEM((devices, 2 * ROWS, HEAD_WIDTH), jnp.bfloat16),
            pltpu.VMEM((x_count, rings, 2 * ROWS, HEAD_WIDTH), jnp.bfloat16),
            pltpu.SemaphoreType.DMA((rings + 1,)),
            pltpu.SemaphoreType.DMA((rings + 1,)),
            pltpu.SemaphoreType.DMA((z_copies,)),
            pltpu.SemaphoreType.DMA((z_copies,)),
            pltpu.SemaphoreType.DMA,
            pltpu.SemaphoreType.DMA,
        ],
        compiler_params=pltpu.CompilerParams(
            collective_id=1, has_side_effects=True, vmem_limit_bytes=24 * 2**20
        ),
    )(tables, grads)


def shards(query, output_gradient, prompt_key_pool, prompt_value_pool, block_tables, lengths):
    share = block_tables.shape[0] // (lax.axis_size("resp") // lax.axis_size("kvh") // 2)
    pages = block_tables.shape[1]
    held = gathered(block_tables, prompt_key_pool, prompt_value_pool, share, pages)
    grad_query, grads = attention_gradients(lengths, query[0], output_gradient[0], held)
    grad_key, grad_value = scattered(block_tables, grads, share, pages)
    return grad_query[None], grad_key, grad_value


def solution(mesh):
    placed = (
        P("resp", None, "kvh"),
        P("resp", None, "kvh"),
        P("resp", "kvh", None),
        P("resp", "kvh", None),
        P(),
        P("resp"),
    )
    return jax.shard_map(
        shards,
        mesh=mesh,
        in_specs=placed,
        out_specs=(P("resp", None, "kvh"), P("resp", "kvh", None), P("resp", "kvh", None)),
        check_vma=False,
    )
```

```python
import functools

import jax
import jax.numpy as jnp
from jax import lax
from jax.experimental import pallas as pl
from jax.experimental.pallas import tpu as pltpu
from jax.sharding import PartitionSpec as P

QUERY_HEADS = 64
KEY_VALUE_HEADS = 8
HEAD_WIDTH = 128
PAGES_DEV = 4
SLOTS = 2
ROWS = 16
MESH = pl.DeviceIdType.MESH
LOG2E = 1.4426950408889634
STEP_ROWS = 512


def place():
    rings = lax.axis_size("kvh")
    own = lax.axis_index("resp")
    head = lax.axis_index("kvh")
    return own, head, own // rings, lax.rem(own, rings), rings


def mod(value, size):
    return lax.rem(value + 2 * size, size)


def local_slots(tables, prompt, own, share, pages):
    first, second, count = jnp.int32(-1), jnp.int32(-1), jnp.int32(0)
    for j in range(pages):
        page = tables[prompt * share, j]
        hit = (page // PAGES_DEV) == own
        local = lax.rem(page, PAGES_DEV)
        first = jnp.where(hit & (count == 0), local, first)
        second = jnp.where(hit & (count == 1), local, second)
        count = count + hit.astype(jnp.int32)
    return first, second


def prompt_owners(tables, prompt, share, pages):
    held = [tables[prompt * share, j] // PAGES_DEV for j in range(pages)]
    ranks = []
    for j in range(pages):
        below = jnp.int32(0)
        for i in range(pages):
            if i != j:
                below = below + (held[i] < held[j]).astype(jnp.int32)
        ranks.append(below // SLOTS)
    owners = []
    for n in range(pages // SLOTS):
        owner = jnp.int32(0)
        for j in range(pages):
            owner = jnp.where(ranks[j] == n, held[j], owner)
        owners.append(owner)
    return owners


def spread_peers(own_x, own_z, head, rings, x_count):
    def target(i):
        dx, dh = i // rings, lax.rem(i, rings)
        x = lax.rem(own_x + dx, x_count)
        h = lax.rem(head + dh, rings)
        z = mod(own_z - dh + 1, rings)
        return x, h, z

    def origin(i):
        dx, dk = i // rings, lax.rem(i, rings)
        x = lax.rem(own_x + dx, x_count)
        k = lax.rem(head + dk, rings)
        z = mod(own_z - dk - 1, rings)
        return x, k, z

    return target, origin


def ring_peers(own_x, own_z, rings):
    right = own_x * rings + lax.rem(own_z + 1, rings)
    left = own_x * rings + mod(own_z - 1, rings)
    buddy = (own_x + 1 - 2 * lax.rem(own_x, 2)) * rings + own_z
    return right, left, buddy


def attention_phase(length, query, upstream, pages, keys_t, work, soft, slopes, query_s, upstream_s, grad_query):
    tokens, width = query.shape
    groups = width // HEAD_WIDTH
    chunks, rows = pages.shape[1], pages.shape[2]
    count = chunks * rows
    step = min(STEP_ROWS, count)
    steps = count // step
    scale = HEAD_WIDTH ** -0.5
    pairs = soft.shape[0]
    pair_rows = soft.shape[1]
    for c in range(chunks):
        keys_t[:, c * rows:(c + 1) * rows] = pages[0, c].T

    def columns(g):
        return pl.ds(g * HEAD_WIDTH, HEAD_WIDTH)

    def lanes(g):
        return pl.ds(g * tokens, tokens)

    def span(n):
        return pl.ds(n * step, step)

    def block(n):
        return pl.ds(n * step // pair_rows, step // pair_rows)

    def held(part, n):
        return pages[part, n * step // rows:(n + 1) * step // rows].reshape(step, HEAD_WIDTH)

    def products(g, n, query_t, upstream_t, top):
        score, slope = work[g % 2]
        part = jnp.dot(held(0, n), query_t, preferred_element_type=jnp.float32) * (scale * LOG2E)
        score[span(n)] = part
        slope[span(n)] = jnp.dot(held(1, n), upstream_t, preferred_element_type=jnp.float32)
        return jnp.maximum(top, jnp.max(part.reshape(-1, 8, tokens), axis=0))

    lowest = jnp.full((8, tokens), -jnp.inf, jnp.float32)
    zero = jnp.zeros((8, tokens), jnp.float32)
    live = lax.broadcasted_iota(jnp.int32, (1, tokens), 1) < length
    query_t, upstream_t = query[:, columns(0)].T, upstream[:, columns(0)].T
    top = lowest
    for n in range(steps):
        top = products(0, n, query_t, upstream_t, top)
    before = None
    for g in range(groups + 1):
        if g < groups:
            score, slope = work[g % 2]
            peak = jnp.max(top, axis=0, keepdims=True)
            total, delta, top = zero, zero, lowest
            if g + 1 < groups:
                next_query, next_upstream = query[:, columns(g + 1)].T, upstream[:, columns(g + 1)].T
            for n in range(steps):
                if g + 1 < groups:
                    top = products(g + 1, n, next_query, next_upstream, top)
                part = jnp.exp2(score[span(n)] - peak)
                score[span(n)] = part
                soft[block(n), :, lanes(g)] = part.astype(jnp.bfloat16).reshape(-1, pair_rows, tokens)
                total = total + jnp.sum(part.reshape(-1, 8, tokens), axis=0)
                delta = delta + jnp.sum((part * slope[span(n)]).reshape(-1, 8, tokens), axis=0)
            inverse = 1.0 / jnp.sum(total, axis=0, keepdims=True)
            delta = jnp.sum(delta, axis=0, keepdims=True) * inverse
            inverse = jnp.where(live, inverse, 0.0)
            query_s[lanes(g)] = (query_t.astype(jnp.float32) * (inverse * scale)).T.astype(jnp.bfloat16)
            upstream_s[lanes(g)] = (upstream_t.astype(jnp.float32) * inverse).T.astype(jnp.bfloat16)
        if before is not None:
            last, factor = before
            spread_slopes = slopes[:, :, lanes(last)].reshape(count, tokens)
            result = jnp.dot(keys_t[...], spread_slopes, preferred_element_type=jnp.float32)
        if g < groups:
            for n in range(steps):
                part = (score[span(n)] * (slope[span(n)] - delta)).astype(jnp.bfloat16)
                slopes[block(n), :, lanes(g)] = part.reshape(-1, pair_rows, tokens)
        if before is not None:
            grad_query[:, columns(last)] = (result * factor).T.astype(jnp.bfloat16)
        if g < groups:
            before = (g, inverse * scale)
            if g + 1 < groups:
                query_t, upstream_t = next_query, next_upstream


def page_gradients(pair, tokens, soft, slopes, query_s, upstream_s, grads):
    groups = query_s.shape[0] // tokens
    for part, (left, right) in enumerate(((slopes, query_s), (soft, upstream_s))):
        value = 0.0
        for g in range(groups):
            lanes = pl.ds(g * tokens, tokens)
            value = value + jnp.dot(left[pair, :, lanes], right[lanes], preferred_element_type=jnp.float32)
        grads[pair, part] = value.reshape(SLOTS, -1, HEAD_WIDTH)


def whole_kernel(share, page_count, tables, lengths, query_hbm, upstream_hbm, key_pool, value_pool,
                 grad_query_hbm, grad_key, grad_value,
                 query, upstream, grad_query, pages, keys_t, score_a, slope_a, score_b, slope_b, soft, slopes,
                 query_s, upstream_s, grads, stage, recv, x_out, x_in, z_out, z_in, total, packed, back_stage, back,
                 copy_sem, spread_send, spread_recv, send_sem, recv_sem, x_send, x_recv, z_send, z_recv,
                 back_send, back_recv):
    own, head, own_x, own_z, rings = place()
    x_count = lax.axis_size("resp") // rings
    target, origin = spread_peers(own_x, own_z, head, rings, x_count)
    right, left, buddy = ring_peers(own_x, own_z, rings)
    messages = x_count * rings
    tokens = query.shape[0]
    side = lax.rem(own_x, 2)
    hops = {1: rings // 2, -1: rings // 2 - 1}
    peers = {1: right, -1: left}

    barrier = pltpu.get_barrier_semaphore()

    def greet(i, carry):
        x, h, z = target(i)
        pl.semaphore_signal(barrier, inc=1, device_id=(x * rings + z, h), device_id_type=MESH)
        x, k, z = origin(i)
        pl.semaphore_signal(barrier, inc=1, device_id=(x * rings + z, k), device_id_type=MESH)
        return carry

    lax.fori_loop(0, messages, greet, 0)
    for peer in (right, left, buddy):
        pl.semaphore_signal(barrier, inc=1, device_id=(peer, head), device_id_type=MESH)

    load_query = pltpu.make_async_copy(query_hbm, query, copy_sem.at[0])
    load_upstream = pltpu.make_async_copy(upstream_hbm, upstream, copy_sem.at[1])
    load_query.start()
    load_upstream.start()
    picked = []
    for prompt in range(x_count // 2):
        picked += local_slots(tables, prompt, own, share, page_count)
    for n, slot in enumerate(picked):
        page = jnp.maximum(slot, 0)
        for h in range(rings):
            columns = slice(h * HEAD_WIDTH, (h + 1) * HEAD_WIDTH)
            stage[n, h, :ROWS, :] = key_pool[page, :, columns]
            stage[n, h, ROWS:, :] = value_pool[page, :, columns]
    pl.semaphore_wait(barrier, 2 * messages + 3)

    def send(i, carry):
        x, h, z = target(i)
        pltpu.make_async_remote_copy(
            src_ref=stage.at[x, h], dst_ref=recv.at[own], send_sem=spread_send, recv_sem=spread_recv,
            device_id=(x * rings + z, h), device_id_type=MESH,
        ).start()
        return carry

    lax.fori_loop(0, messages, send, 0)
    owners = prompt_owners(tables, own_x // 2, share, page_count)
    pltpu.make_async_copy(recv, recv, spread_recv).wait()

    mine = 2 * own_z + side
    for n, owner in enumerate(owners):
        piece = recv[owner]
        pages[0, mine, n * ROWS:(n + 1) * ROWS, :] = piece[:ROWS]
        pages[1, mine, n * ROWS:(n + 1) * ROWS, :] = piece[ROWS:]

    copies = []
    moving = {}

    def push(name, chunk, part, peer):
        slot = len(moving)
        copy = pltpu.make_async_remote_copy(
            src_ref=pages.at[part, chunk], dst_ref=pages.at[part, chunk],
            send_sem=send_sem.at[slot], recv_sem=recv_sem.at[slot],
            device_id=(peer, head), device_id_type=MESH,
        )
        copy.start()
        copies.append(copy)
        moving[name] = copy

    push(("x", 1), mine, 1, buddy)
    for way in (1, -1):
        for part in (0, 1):
            push(("z", way, 0, part, 0), mine, part, peers[way])
    push(("x", 0, 0), mine, 0, buddy)
    moving["x", 1].wait_recv()
    for way in (1, -1):
        push(("z", way, 0, 1, 1), 2 * own_z + 1 - side, 1, peers[way])
    for step in range(1, rings // 2 + 1):
        for part, flip in ((0, 0), (1, 0), (1, 1)):
            for way in (1, -1):
                if step > hops[way]:
                    continue
                moving["z", way, step - 1, part, flip].wait_recv()
                chunk = 2 * mod(own_z - way * step, rings) + (1 - side if flip else side)
                if step < hops[way]:
                    push(("z", way, step, part, flip), chunk, part, peers[way])
                if part == 0:
                    push(("x", 0, way * step), chunk, part, buddy)
    for name, copy in moving.items():
        if name[0] == "x" and name[1] == 0:
            copy.wait_recv()

    load_query.wait()
    load_upstream.wait()
    attention_phase(lengths[0], query, upstream, pages, keys_t, ((score_a, slope_a), (score_b, slope_b)),
                    soft, slopes, query_s, upstream_s, grad_query)
    store_query = pltpu.make_async_copy(grad_query, grad_query_hbm, copy_sem.at[0])
    store_query.start()

    order = []
    for step in range(rings // 2):
        order += [way * (hops[way] - step) for way in (1, -1) if step < hops[way]]
    order.append(0)
    x_moving, z_moving = {}, {}

    def x_push(n):
        copy = pltpu.make_async_remote_copy(
            src_ref=x_out.at[n], dst_ref=x_in.at[n], send_sem=x_send.at[n], recv_sem=x_recv.at[n],
            device_id=(buddy, head), device_id_type=MESH,
        )
        copy.start()
        copies.append(copy)
        x_moving[n] = copy

    def own_term(item, d):
        spot = mod(own_z + d, rings)
        if item == 0:
            n = order.index(d)
            x_moving[n].wait_recv()
            return grads[spot, 0, side] + x_in[n].astype(jnp.float32)
        return grads[spot, 1, side if item == 1 else 1 - side]

    def z_arrived(way, step, item):
        copy, n = z_moving[way, step, item]
        copy.wait_recv()
        return z_in[n].astype(jnp.float32)

    def z_push(item, d):
        way = 1 if d > 0 else -1
        step = hops[way] - abs(d)
        value = own_term(item, d)
        if step > 0:
            value = value + z_arrived(way, step - 1, item)
        n = (way == -1) * 3 * hops[1] + step * 3 + item
        z_out[n] = value.astype(jnp.bfloat16)
        copy = pltpu.make_async_remote_copy(
            src_ref=z_out.at[n], dst_ref=z_in.at[n], send_sem=z_send.at[n], recv_sem=z_recv.at[n],
            device_id=(peers[way], head), device_id_type=MESH,
        )
        copy.start()
        copies.append(copy)
        z_moving[way, step, item] = (copy, n)

    def finish(item):
        value = own_term(item, 0)
        for way in (1, -1):
            if hops[way]:
                value = value + z_arrived(way, hops[way] - 1, item)
        return value

    for n, d in enumerate(order):
        spot = mod(own_z + d, rings)
        page_gradients(spot, tokens, soft, slopes, query_s, upstream_s, grads)
        x_out[n] = grads[spot, 0, 1 - side].astype(jnp.bfloat16)
        x_push(n)
        if d != 0:
            z_push(1, d)
            z_push(2, d)
        if n > 0:
            z_push(0, order[n - 1])
    x_out[rings] = finish(2).astype(jnp.bfloat16)
    x_push(rings)
    total[0] = finish(0)
    value_total = finish(1)
    x_moving[rings].wait_recv()
    total[1] = value_total + x_in[rings].astype(jnp.float32)

    for n in range(rings):
        packed[n, :ROWS, :] = total[0, n * ROWS:(n + 1) * ROWS, :].astype(jnp.bfloat16)
        packed[n, ROWS:, :] = total[1, n * ROWS:(n + 1) * ROWS, :].astype(jnp.bfloat16)
    for device in range(x_count * rings):
        rank = jnp.int32(0)
        for n, owner in enumerate(owners):
            rank = jnp.where(owner == device, n, rank)
        back_stage[device] = packed[rank]

    def send_back(i, carry):
        x, k, z = origin(i)
        pltpu.make_async_remote_copy(
            src_ref=back_stage.at[x * rings + z], dst_ref=back.at[own_x, head],
            send_sem=back_send, recv_sem=back_recv,
            device_id=(x * rings + z, k), device_id_type=MESH,
        ).start()
        return carry

    lax.fori_loop(0, messages, send_back, 0)
    pltpu.make_async_copy(back, back, back_recv).wait()
    for page in range(PAGES_DEV):
        takes = [(slot == page).astype(jnp.float32) for slot in picked]
        for h in range(rings):
            columns = slice(h * HEAD_WIDTH, (h + 1) * HEAD_WIDTH)
            value = jnp.zeros((2 * ROWS, HEAD_WIDTH), jnp.float32)
            for n, take in enumerate(takes):
                value = value + back[n, h].astype(jnp.float32) * take
            grad_key[page, :, columns] = value[:ROWS]
            grad_value[page, :, columns] = value[ROWS:]
    for copy in copies:
        copy.wait_send()
    pltpu.make_async_copy(stage, stage, spread_send).wait()
    pltpu.make_async_copy(back_stage, back_stage, back_send).wait()
    store_query.wait()


def gradients(tables, lengths, query, upstream, key_pool, value_pool):
    rings = lax.axis_size("kvh")
    devices = lax.axis_size("resp")
    x_count = devices // rings
    share = 2 * rings
    page_count = tables.shape[1]
    tokens, width = query.shape
    rows = rings * ROWS
    chunks = SLOTS * rings
    count = chunks * rows
    query_rows = tokens * (width // HEAD_WIDTH)
    z_copies = 3 * (rings - 1)
    gathers = 1 + rings + z_copies
    out = jax.ShapeDtypeStruct((PAGES_DEV, ROWS, rings * HEAD_WIDTH), jnp.float32)
    bf16, f32 = jnp.bfloat16, jnp.float32
    vmem = pl.BlockSpec(memory_space=pltpu.VMEM)
    smem = pl.BlockSpec(memory_space=pltpu.SMEM)
    anywhere = pl.BlockSpec(memory_space=pl.ANY)
    dma = pltpu.SemaphoreType.DMA
    return pl.pallas_call(
        functools.partial(whole_kernel, share, page_count),
        out_shape=(jax.ShapeDtypeStruct(query.shape, bf16), out, out),
        in_specs=[smem, smem, anywhere, anywhere, vmem, vmem],
        out_specs=(anywhere, vmem, vmem),
        scratch_shapes=[
            pltpu.VMEM((tokens, width), bf16),
            pltpu.VMEM((tokens, width), bf16),
            pltpu.VMEM((tokens, width), bf16),
            pltpu.VMEM((2, chunks, rows, HEAD_WIDTH), bf16),
            pltpu.VMEM((HEAD_WIDTH, count), bf16),
            pltpu.VMEM((count, tokens), f32),
            pltpu.VMEM((count, tokens), f32),
            pltpu.VMEM((count, tokens), f32),
            pltpu.VMEM((count, tokens), f32),
            pltpu.VMEM((rings, 2 * rows, query_rows), bf16),
            pltpu.VMEM((rings, 2 * rows, query_rows), bf16),
            pltpu.VMEM((query_rows, HEAD_WIDTH), bf16),
            pltpu.VMEM((query_rows, HEAD_WIDTH), bf16),
            pltpu.VMEM((rings, 2, SLOTS, rows, HEAD_WIDTH), f32),
            pltpu.VMEM((x_count, rings, 2 * ROWS, HEAD_WIDTH), bf16),
            pltpu.VMEM((devices, 2 * ROWS, HEAD_WIDTH), bf16),
            pltpu.VMEM((rings + 1, rows, HEAD_WIDTH), bf16),
            pltpu.VMEM((rings + 1, rows, HEAD_WIDTH), bf16),
            pltpu.VMEM((z_copies, rows, HEAD_WIDTH), bf16),
            pltpu.VMEM((z_copies, rows, HEAD_WIDTH), bf16),
            pltpu.VMEM((2, rows, HEAD_WIDTH), f32),
            pltpu.VMEM((rings, 2 * ROWS, HEAD_WIDTH), bf16),
            pltpu.VMEM((devices, 2 * ROWS, HEAD_WIDTH), bf16),
            pltpu.VMEM((x_count, rings, 2 * ROWS, HEAD_WIDTH), bf16),
            dma((2,)),
            dma,
            dma,
            dma((gathers,)),
            dma((gathers,)),
            dma((rings + 1,)),
            dma((rings + 1,)),
            dma((z_copies,)),
            dma((z_copies,)),
            dma,
            dma,
        ],
        compiler_params=pltpu.CompilerParams(
            collective_id=0, has_side_effects=True, vmem_limit_bytes=48 * 2**20
        ),
    )(tables, lengths, query, upstream, key_pool, value_pool)


def shards(query, output_gradient, prompt_key_pool, prompt_value_pool, block_tables, lengths):
    grad_query, grad_key, grad_value = gradients(
        block_tables, lengths, query[0], output_gradient[0], prompt_key_pool, prompt_value_pool
    )
    return grad_query[None], grad_key, grad_value


def solution(mesh):
    placed = (
        P("resp", None, "kvh"),
        P("resp", None, "kvh"),
        P("resp", "kvh", None),
        P("resp", "kvh", None),
        P(),
        P("resp"),
    )
    return jax.shard_map(
        shards,
        mesh=mesh,
        in_specs=placed,
        out_specs=(P("resp", None, "kvh"), P("resp", "kvh", None), P("resp", "kvh", None)),
        check_vma=False,
    )
```

```python
import functools

import jax
import jax.numpy as jnp
from jax import lax
from jax.experimental import pallas as pl
from jax.experimental.pallas import tpu as pltpu
from jax.sharding import PartitionSpec as P

QUERY_HEADS = 64
KEY_VALUE_HEADS = 8
HEAD_WIDTH = 128
PAGES_DEV = 4
SLOTS = 2
ROWS = 16
MESH = pl.DeviceIdType.MESH
LOG2E = 1.4426950408889634
STEP_ROWS = 512


def place():
    rings = lax.axis_size("kvh")
    own = lax.axis_index("resp")
    head = lax.axis_index("kvh")
    return own, head, own // rings, lax.rem(own, rings), rings


def mod(value, size):
    return lax.rem(value + 2 * size, size)


def local_slots(tables, prompt, own, share, pages):
    first, second, count = jnp.int32(-1), jnp.int32(-1), jnp.int32(0)
    for j in range(pages):
        page = tables[prompt * share, j]
        hit = (page // PAGES_DEV) == own
        local = lax.rem(page, PAGES_DEV)
        first = jnp.where(hit & (count == 0), local, first)
        second = jnp.where(hit & (count == 1), local, second)
        count = count + hit.astype(jnp.int32)
    return first, second


def prompt_owners(tables, prompt, share, pages):
    held = [tables[prompt * share, j] // PAGES_DEV for j in range(pages)]
    ranks = []
    for j in range(pages):
        below = jnp.int32(0)
        for i in range(pages):
            if i != j:
                below = below + (held[i] < held[j]).astype(jnp.int32)
        ranks.append(below // SLOTS)
    owners = []
    for n in range(pages // SLOTS):
        owner = jnp.int32(0)
        for j in range(pages):
            owner = jnp.where(ranks[j] == n, held[j], owner)
        owners.append(owner)
    return owners


def spread_peers(own_x, own_z, head, rings, x_count):
    def target(i):
        dx, dh = i // rings, lax.rem(i, rings)
        x = lax.rem(own_x + dx, x_count)
        h = lax.rem(head + dh, rings)
        z = mod(own_z - dh + 1, rings)
        return x, h, z

    def origin(i):
        dx, dk = i // rings, lax.rem(i, rings)
        x = lax.rem(own_x + dx, x_count)
        k = lax.rem(head + dk, rings)
        z = mod(own_z - dk - 1, rings)
        return x, k, z

    return target, origin


def attention_phase(length, query, upstream, pages, keys_t, work, turned, soft, slopes, query_s, upstream_s, grad_query):
    tokens, width = query.shape
    groups = width // HEAD_WIDTH
    chunks, rows = pages.shape[1], pages.shape[2]
    count = chunks * rows
    step = min(STEP_ROWS, count)
    steps = count // step
    scale = HEAD_WIDTH ** -0.5
    pair_rows = soft.shape[1]
    for c in range(chunks):
        keys_t[:, c * rows:(c + 1) * rows] = pages[0, c].T

    def columns(g):
        return pl.ds(pl.multiple_of(g * HEAD_WIDTH, HEAD_WIDTH), HEAD_WIDTH)

    def lanes(g):
        return pl.ds(pl.multiple_of(g * tokens, tokens), tokens)

    def span(n):
        return pl.ds(n * step, step)

    def block(n):
        return pl.ds(n * step // pair_rows, step // pair_rows)

    def held(part, n):
        return pages[part, n * step // rows:(n + 1) * step // rows].reshape(step, HEAD_WIDTH)

    lowest = jnp.full((8, tokens), -jnp.inf, jnp.float32)
    zero = jnp.zeros((8, tokens), jnp.float32)
    live = lax.broadcasted_iota(jnp.int32, (1, tokens), 1) < length

    def turn(g, side):
        query_t, upstream_t = turned[side]
        query_t[...] = query[:, columns(g)].T
        upstream_t[...] = upstream[:, columns(g)].T

    def products(side, n, top):
        query_t, upstream_t = turned[side]
        score, slope = work[side]
        part = jnp.dot(held(0, n), query_t[...], preferred_element_type=jnp.float32) * (scale * LOG2E)
        score[span(n)] = part
        slope[span(n)] = jnp.dot(held(1, n), upstream_t[...], preferred_element_type=jnp.float32)
        return jnp.maximum(top, jnp.max(part.reshape(-1, 8, tokens), axis=0))

    def query_products(g):
        block_slopes = slopes[:, :, lanes(g)].reshape(count, tokens)
        return jnp.dot(keys_t[...], block_slopes, preferred_element_type=jnp.float32)

    def one_group(g, side, top, before, factor, after):
        score, slope = work[side]
        peak = jnp.max(top, axis=0, keepdims=True)
        total, delta, top = zero, zero, lowest
        turn(after, 1 - side)
        for n in range(steps):
            top = products(1 - side, n, top)
            part = jnp.exp2(score[span(n)] - peak)
            score[span(n)] = part
            soft[block(n), :, lanes(g)] = part.astype(jnp.bfloat16).reshape(-1, pair_rows, tokens)
            total = total + jnp.sum(part.reshape(-1, 8, tokens), axis=0)
            delta = delta + jnp.sum((part * slope[span(n)]).reshape(-1, 8, tokens), axis=0)
        inverse = 1.0 / jnp.sum(total, axis=0, keepdims=True)
        delta = jnp.sum(delta, axis=0, keepdims=True) * inverse
        inverse = jnp.where(live, inverse, 0.0)
        query_t, upstream_t = turned[side]
        query_s[lanes(g)] = (query_t[...].astype(jnp.float32) * (inverse * scale)).T.astype(jnp.bfloat16)
        upstream_s[lanes(g)] = (upstream_t[...].astype(jnp.float32) * inverse).T.astype(jnp.bfloat16)
        result = query_products(before)
        for n in range(steps):
            part = (score[span(n)] * (slope[span(n)] - delta)).astype(jnp.bfloat16)
            slopes[block(n), :, lanes(g)] = part.reshape(-1, pair_rows, tokens)
        grad_query[:, columns(before)] = (result * factor).T.astype(jnp.bfloat16)
        return top, inverse * scale

    final = groups - 1
    slopes[:, :, final * tokens:] = jnp.zeros((slopes.shape[0], pair_rows, tokens), jnp.bfloat16)
    turn(0, 0)
    top = lowest
    for n in range(steps):
        top = products(0, n, top)

    def two_groups(i, carry):
        top, factor = carry
        g = 2 * i
        top, factor = one_group(g, 0, top, lax.rem(g + final, groups), factor, g + 1)
        return one_group(g + 1, 1, top, g, factor, lax.rem(g + 2, groups))

    top, factor = lax.fori_loop(0, groups // 2, two_groups, (top, jnp.zeros((1, tokens), jnp.float32)))
    grad_query[:, final * HEAD_WIDTH:] = (query_products(final) * factor).T.astype(jnp.bfloat16)


def page_gradients(pair, tokens, soft, slopes, query_s, upstream_s, grads):
    groups = query_s.shape[0] // tokens
    for part, (left, right) in enumerate(((slopes, query_s), (soft, upstream_s))):
        value = 0.0
        for g in range(groups):
            lanes = pl.ds(g * tokens, tokens)
            value = value + jnp.dot(left[pair, :, lanes], right[lanes], preferred_element_type=jnp.float32)
        grads[pair, part] = value.reshape(SLOTS, -1, HEAD_WIDTH)


def whole_kernel(share, page_count, tables, lengths, query_hbm, upstream_hbm, key_hbm, value_hbm,
                 grad_query_hbm, grad_key, grad_value,
                 key_pool, value_pool, ranks, query, upstream, grad_query, pages, keys_t, query_a, upstream_a,
                 query_b, upstream_b, score_a, slope_a, score_b, slope_b, soft, slopes,
                 query_s, upstream_s, grads, stage, recv, x_out, x_in, z_out, z_in, total, packed, back_stage, back,
                 copy_sem, spread_send, spread_recv, send_sem, recv_sem, x_send, x_recv, z_send, z_recv,
                 back_send, back_recv):
    own, head, own_x, own_z, rings = place()
    x_count = lax.axis_size("resp") // rings
    target, origin = spread_peers(own_x, own_z, head, rings, x_count)
    buddy = (own_x + 1 - 2 * lax.rem(own_x, 2)) * rings + own_z

    def ring(d):
        return own_x * rings + mod(own_z + d, rings)

    neighbours = [buddy] + [ring(d) for d in ((1, -1, 2, -2) if rings > 4 else (1, -1, 2))]
    messages = x_count * rings
    tokens = query.shape[0]
    side = lax.rem(own_x, 2)
    half = rings // 2
    loads = [
        pltpu.make_async_copy(source, place, copy_sem.at[n])
        for n, (source, place) in enumerate(
            ((key_hbm, key_pool), (value_hbm, value_pool), (query_hbm, query), (upstream_hbm, upstream))
        )
    ]
    for load in loads:
        load.start()
    barrier = pltpu.get_barrier_semaphore()

    def greet(i, carry):
        x, h, z = target(i)
        pl.semaphore_signal(barrier, inc=1, device_id=(x * rings + z, h), device_id_type=MESH)
        x, k, z = origin(i)
        pl.semaphore_signal(barrier, inc=1, device_id=(x * rings + z, k), device_id_type=MESH)
        return carry

    lax.fori_loop(0, messages, greet, 0)
    for peer in neighbours:
        pl.semaphore_signal(barrier, inc=1, device_id=(peer, head), device_id_type=MESH)

    picked = []
    for prompt in range(x_count // 2):
        picked += local_slots(tables, prompt, own, share, page_count)
    loads[0].wait()
    loads[1].wait()
    for n, slot in enumerate(picked):
        page = jnp.maximum(slot, 0)
        for h in range(rings):
            columns = slice(h * HEAD_WIDTH, (h + 1) * HEAD_WIDTH)
            stage[n, h, :ROWS, :] = key_pool[page, :, columns]
            stage[n, h, ROWS:, :] = value_pool[page, :, columns]
    pl.semaphore_wait(barrier, 2 * messages + len(neighbours))

    def send(i, carry):
        x, h, z = target(i)
        pltpu.make_async_remote_copy(
            src_ref=stage.at[x, h], dst_ref=recv.at[own], send_sem=spread_send, recv_sem=spread_recv,
            device_id=(x * rings + z, h), device_id_type=MESH,
        ).start()
        return carry

    lax.fori_loop(0, messages, send, 0)
    owners = prompt_owners(tables, own_x // 2, share, page_count)
    for device in range(x_count * rings):
        rank = jnp.int32(0)
        for n, owner in enumerate(owners):
            rank = jnp.where(owner == device, n, rank)
        ranks[device] = rank
    pltpu.make_async_copy(recv, recv, spread_recv).wait()

    mine = 2 * own_z + side
    for n, owner in enumerate(owners):
        piece = recv[owner]
        pages[0, mine, n * ROWS:(n + 1) * ROWS, :] = piece[:ROWS]
        pages[1, mine, n * ROWS:(n + 1) * ROWS, :] = piece[ROWS:]

    copies = []
    moving = {}

    def push(name, chunk, part, peer):
        slot = len(moving)
        copy = pltpu.make_async_remote_copy(
            src_ref=pages.at[part, chunk], dst_ref=pages.at[part, chunk],
            send_sem=send_sem.at[slot], recv_sem=recv_sem.at[slot],
            device_id=(peer, head), device_id_type=MESH,
        )
        copy.start()
        copies.append(copy)
        moving[name] = copy

    def relay(d, part):
        way = 1 if d > 0 else -1
        chunk = 2 * mod(own_z - d, rings) + side
        push(("z", d + way, part), chunk, part, ring(way))
        if part == (0 if way > 0 else 1):
            push(("z", half, part), chunk, part, ring(2 * way))

    for part in (0, 1):
        push(("x", part, 0), mine, part, buddy)
    for d in ((2, -2, 1, -1) if half == 4 else (2, 1, -1)):
        for part in (0, 1):
            push(("z", d, part), mine, part, ring(d))
    for d in ((2, -2, 0, 3, -3, 4, 1, -1) if half == 4 else (0, 2, 1, -1)):
        for part in (0, 1):
            if d == 0:
                moving["x", part, 0].wait_recv()
                for near in (1, -1):
                    push(("w", near, part), 2 * own_z + 1 - side, part, ring(near))
                continue
            moving["z", d, part].wait_recv()
            if half == 4 and abs(d) == 2:
                relay(d, part)
            if abs(d) > 1:
                push(("x", part, d), 2 * mod(own_z - d, rings) + side, part, buddy)
    for name, copy in moving.items():
        if name[0] == "w" or name[0] == "x" and name[2] != 0:
            copy.wait_recv()

    loads[2].wait()
    loads[3].wait()
    attention_phase(lengths[0], query, upstream, pages, keys_t, ((score_a, slope_a), (score_b, slope_b)),
                    ((query_a, upstream_a), (query_b, upstream_b)), soft, slopes, query_s, upstream_s, grad_query)
    store_query = pltpu.make_async_copy(grad_query, grad_query_hbm, copy_sem.at[0])
    store_query.start()

    far = [4, 3, -3, 2, -2] if half == 4 else [2]
    x_moving, z_moving = {}, {}

    def x_push(n, d, added):
        for part in (0, 1):
            value = grads[mod(own_z + d, rings), part, 1 - side]
            for term in added:
                value = value + z_arrived(term, part)
            x_out[n, part] = value.astype(jnp.bfloat16)
        copy = pltpu.make_async_remote_copy(
            src_ref=x_out.at[n], dst_ref=x_in.at[n], send_sem=x_send.at[n], recv_sem=x_recv.at[n],
            device_id=(buddy, head), device_id_type=MESH,
        )
        copy.start()
        copies.append(copy)
        x_moving[n] = copy

    def z_arrived(name, part):
        copy, n = z_moving[name, part]
        copy.wait_recv()
        return z_in[n].astype(jnp.float32)

    def z_push(name, part, value, device):
        n = len(z_moving)
        z_out[n] = value.astype(jnp.bfloat16)
        copy = pltpu.make_async_remote_copy(
            src_ref=z_out.at[n], dst_ref=z_in.at[n], send_sem=z_send.at[n], recv_sem=z_recv.at[n],
            device_id=(device, head), device_id_type=MESH,
        )
        copy.start()
        copies.append(copy)
        z_moving[name, part] = (copy, n)

    def far_push(d):
        n = far.index(d)
        way = 1 if d > 0 else -1
        x_moving[n].wait_recv()
        for part in (0, 1):
            value = grads[mod(own_z + d, rings), part, side] + x_in[n, part].astype(jnp.float32)
            if half == 4 and abs(d) == 2:
                value = value + z_arrived(("far", 3 * way), part)
                if part == (0 if way > 0 else 1):
                    value = value + z_arrived(("far", 4), part)
            if abs(d) == 2:
                z_push(("far", d), part, value, ring(d))
            elif abs(d) == 3:
                z_push(("far", d), part, value, ring(way))
            else:
                z_push(("far", d), part, value, ring(2 if part == 0 else -2))

    def near_push(d):
        for flip in (0, 1):
            for part in (0, 1):
                value = grads[mod(own_z + d, rings), part, 1 - side if flip else side]
                z_push(("near", d, flip), part, value, ring(d))

    def compute(d):
        page_gradients(mod(own_z + d, rings), tokens, soft, slopes, query_s, upstream_s, grads)

    for n, d in enumerate(far):
        compute(d)
        x_push(n, d, ())
    early = [d for d in far if abs(d) > 2]
    late = [d for d in far if abs(d) == 2]
    for n, d in enumerate((1, -1, 0)):
        compute(d)
        if d != 0:
            near_push(d)
        if n < len(early):
            far_push(early[n])
    x_push(len(far), 0, (("near", 1, 1), ("near", -1, 1)))
    for d in late:
        far_push(d)
    for part in (0, 1):
        value = grads[own_z, part, side]
        for name in [("near", 1, 0), ("near", -1, 0)] + [("far", d) for d in late]:
            value = value + z_arrived(name, part)
        if part == 0:
            x_moving[len(far)].wait_recv()
        total[part] = value + x_in[len(far), part].astype(jnp.float32)

    for n in range(rings):
        packed[n, :ROWS, :] = total[0, n * ROWS:(n + 1) * ROWS, :].astype(jnp.bfloat16)
        packed[n, ROWS:, :] = total[1, n * ROWS:(n + 1) * ROWS, :].astype(jnp.bfloat16)
    for device in range(x_count * rings):
        back_stage[device] = packed[ranks[device]]

    def send_back(i, carry):
        x, k, z = origin(i)
        pltpu.make_async_remote_copy(
            src_ref=back_stage.at[x * rings + z], dst_ref=back.at[own_x, head],
            send_sem=back_send, recv_sem=back_recv,
            device_id=(x * rings + z, k), device_id_type=MESH,
        ).start()
        return carry

    lax.fori_loop(0, messages, send_back, 0)
    pltpu.make_async_copy(back, back, back_recv).wait()
    for page in range(PAGES_DEV):
        takes = [(slot == page).astype(jnp.float32) for slot in picked]
        for h in range(rings):
            columns = slice(h * HEAD_WIDTH, (h + 1) * HEAD_WIDTH)
            value = jnp.zeros((2 * ROWS, HEAD_WIDTH), jnp.float32)
            for n, take in enumerate(takes):
                value = value + back[n, h].astype(jnp.float32) * take
            grad_key[page, :, columns] = value[:ROWS]
            grad_value[page, :, columns] = value[ROWS:]
    for copy in copies:
        copy.wait_send()
    pltpu.make_async_copy(stage, stage, spread_send).wait()
    pltpu.make_async_copy(back_stage, back_stage, back_send).wait()
    store_query.wait()


def gradients(tables, lengths, query, upstream, key_pool, value_pool):
    rings = lax.axis_size("kvh")
    devices = lax.axis_size("resp")
    x_count = devices // rings
    share = 2 * rings
    page_count = tables.shape[1]
    tokens, width = query.shape
    rows = rings * ROWS
    chunks = SLOTS * rings
    count = chunks * rows
    query_rows = tokens * (width // HEAD_WIDTH)
    z_copies = 2 * rings + 2
    gathers = 4 * rings - 2
    out = jax.ShapeDtypeStruct((PAGES_DEV, ROWS, rings * HEAD_WIDTH), jnp.float32)
    bf16, f32 = jnp.bfloat16, jnp.float32
    vmem = pl.BlockSpec(memory_space=pltpu.VMEM)
    smem = pl.BlockSpec(memory_space=pltpu.SMEM)
    anywhere = pl.BlockSpec(memory_space=pl.ANY)
    dma = pltpu.SemaphoreType.DMA
    return pl.pallas_call(
        functools.partial(whole_kernel, share, page_count),
        out_shape=(jax.ShapeDtypeStruct(query.shape, bf16), out, out),
        in_specs=[smem, smem, anywhere, anywhere, anywhere, anywhere],
        out_specs=(anywhere, vmem, vmem),
        scratch_shapes=[
            pltpu.VMEM(key_pool.shape, bf16),
            pltpu.VMEM(key_pool.shape, bf16),
            pltpu.SMEM((devices,), jnp.int32),
            pltpu.VMEM((tokens, width), bf16),
            pltpu.VMEM((tokens, width), bf16),
            pltpu.VMEM((tokens, width), bf16),
            pltpu.VMEM((2, chunks, rows, HEAD_WIDTH), bf16),
            pltpu.VMEM((HEAD_WIDTH, count), bf16),
            pltpu.VMEM((HEAD_WIDTH, tokens), bf16),
            pltpu.VMEM((HEAD_WIDTH, tokens), bf16),
            pltpu.VMEM((HEAD_WIDTH, tokens), bf16),
            pltpu.VMEM((HEAD_WIDTH, tokens), bf16),
            pltpu.VMEM((count, tokens), f32),
            pltpu.VMEM((count, tokens), f32),
            pltpu.VMEM((count, tokens), f32),
            pltpu.VMEM((count, tokens), f32),
            pltpu.VMEM((rings, 2 * rows, query_rows), bf16),
            pltpu.VMEM((rings, 2 * rows, query_rows), bf16),
            pltpu.VMEM((query_rows, HEAD_WIDTH), bf16),
            pltpu.VMEM((query_rows, HEAD_WIDTH), bf16),
            pltpu.VMEM((rings, 2, SLOTS, rows, HEAD_WIDTH), f32),
            pltpu.VMEM((x_count, rings, 2 * ROWS, HEAD_WIDTH), bf16),
            pltpu.VMEM((devices, 2 * ROWS, HEAD_WIDTH), bf16),
            pltpu.VMEM((rings - 2, 2, rows, HEAD_WIDTH), bf16),
            pltpu.VMEM((rings - 2, 2, rows, HEAD_WIDTH), bf16),
            pltpu.VMEM((z_copies, rows, HEAD_WIDTH), bf16),
            pltpu.VMEM((z_copies, rows, HEAD_WIDTH), bf16),
            pltpu.VMEM((2, rows, HEAD_WIDTH), f32),
            pltpu.VMEM((rings, 2 * ROWS, HEAD_WIDTH), bf16),
            pltpu.VMEM((devices, 2 * ROWS, HEAD_WIDTH), bf16),
            pltpu.VMEM((x_count, rings, 2 * ROWS, HEAD_WIDTH), bf16),
            dma((4,)),
            dma,
            dma,
            dma((gathers,)),
            dma((gathers,)),
            dma((rings - 2,)),
            dma((rings - 2,)),
            dma((z_copies,)),
            dma((z_copies,)),
            dma,
            dma,
        ],
        compiler_params=pltpu.CompilerParams(
            collective_id=0, has_side_effects=True, vmem_limit_bytes=60 * 2**20
        ),
    )(tables, lengths, query, upstream, key_pool, value_pool)


def shards(query, output_gradient, prompt_key_pool, prompt_value_pool, block_tables, lengths):
    grad_query, grad_key, grad_value = gradients(
        block_tables, lengths, query[0], output_gradient[0], prompt_key_pool, prompt_value_pool
    )
    return grad_query[None], grad_key, grad_value


def solution(mesh):
    placed = (
        P("resp", None, "kvh"),
        P("resp", None, "kvh"),
        P("resp", "kvh", None),
        P("resp", "kvh", None),
        P(),
        P("resp"),
    )
    return jax.shard_map(
        shards,
        mesh=mesh,
        in_specs=placed,
        out_specs=(P("resp", None, "kvh"), P("resp", "kvh", None), P("resp", "kvh", None)),
        check_vma=False,
    )
```

```python
import functools

import jax
import jax.numpy as jnp
from jax import lax
from jax.experimental import pallas as pl
from jax.experimental.pallas import tpu as pltpu
from jax.sharding import PartitionSpec as P

QUERY_HEADS = 64
KEY_VALUE_HEADS = 8
HEAD_WIDTH = 128
PAGES_DEV = 4
SLOTS = 2
ROWS = 16
MESH = pl.DeviceIdType.MESH
LOG2E = 1.4426950408889634
STEP_ROWS = 512


def place():
    rings = lax.axis_size("kvh")
    own = lax.axis_index("resp")
    head = lax.axis_index("kvh")
    return own, head, own // rings, lax.rem(own, rings), rings


def mod(value, size):
    return lax.rem(value + 2 * size, size)


def local_slots(tables, prompt, own, share, pages):
    first, second, count = jnp.int32(-1), jnp.int32(-1), jnp.int32(0)
    for j in range(pages):
        page = tables[j, prompt * share]
        hit = (page // PAGES_DEV) == own
        local = lax.rem(page, PAGES_DEV)
        first = jnp.where(hit & (count == 0), local, first)
        second = jnp.where(hit & (count == 1), local, second)
        count = count + hit.astype(jnp.int32)
    return first, second


def prompt_owners(tables, prompt, share, pages):
    held = [tables[j, prompt * share] // PAGES_DEV for j in range(pages)]
    ranks = []
    for j in range(pages):
        below = jnp.int32(0)
        for i in range(pages):
            if i != j:
                below = below + (held[i] < held[j]).astype(jnp.int32)
        ranks.append(below // SLOTS)
    owners = []
    for n in range(pages // SLOTS):
        owner = jnp.int32(0)
        for j in range(pages):
            owner = jnp.where(ranks[j] == n, held[j], owner)
        owners.append(owner)
    return owners


def spread_peers(own_x, own_z, head, rings, x_count):
    def around(n, middle, size):
        return mod(middle + (1 - 2 * lax.rem(n, 2)) * ((n + 1) // 2), size)

    def target(i):
        dx, dh = around(lax.rem(i, x_count), x_count // 2, x_count), around(i // x_count, rings // 2 + 1, rings)
        x = lax.rem(own_x + dx, x_count)
        h = lax.rem(head + dh, rings)
        z = mod(own_z - dh + 1, rings)
        return x, h, z

    def origin(i):
        dx, dk = around(lax.rem(i, x_count), x_count // 2, x_count), around(i // x_count, rings // 2 - 1, rings)
        x = lax.rem(own_x + dx, x_count)
        k = lax.rem(head + dk, rings)
        z = mod(own_z - dk - 1, rings)
        return x, k, z

    return target, origin


def attention_phase(length, query, upstream, pages, keys_t, work, turned, soft, slopes, query_s, upstream_s, grad_query):
    tokens, width = query.shape
    groups = width // HEAD_WIDTH
    chunks, rows = pages.shape[1], pages.shape[2]
    count = chunks * rows
    step = min(STEP_ROWS, count)
    steps = count // step
    scale = HEAD_WIDTH ** -0.5
    pair_rows = soft.shape[1]
    for c in range(chunks):
        keys_t[:, c * rows:(c + 1) * rows] = pages[0, c].T

    def columns(g):
        return pl.ds(pl.multiple_of(g * HEAD_WIDTH, HEAD_WIDTH), HEAD_WIDTH)

    def lanes(g):
        return pl.ds(pl.multiple_of(g * tokens, tokens), tokens)

    def span(n):
        return pl.ds(n * step, step)

    def block(n):
        return pl.ds(n * step // pair_rows, step // pair_rows)

    def held(part, n):
        return pages[part, n * step // rows:(n + 1) * step // rows].reshape(step, HEAD_WIDTH)

    lowest = jnp.full((8, tokens), -jnp.inf, jnp.float32)
    zero = jnp.zeros((8, tokens), jnp.float32)
    live = lax.broadcasted_iota(jnp.int32, (1, tokens), 1) < length

    def turn(g, side):
        query_t, upstream_t = turned[side]
        query_t[...] = query[:, columns(g)].T
        upstream_t[...] = upstream[:, columns(g)].T

    def products(side, n, top):
        query_t, upstream_t = turned[side]
        score, slope = work[side]
        part = jnp.dot(held(0, n), query_t[...], preferred_element_type=jnp.float32) * (scale * LOG2E)
        score[span(n)] = part
        slope[span(n)] = jnp.dot(held(1, n), upstream_t[...], preferred_element_type=jnp.float32)
        return jnp.maximum(top, jnp.max(part.reshape(-1, 8, tokens), axis=0))

    def query_products(g):
        block_slopes = slopes[:, :, lanes(g)].reshape(count, tokens)
        return jnp.dot(keys_t[...], block_slopes, preferred_element_type=jnp.float32)

    def one_group(g, side, top, before, factor, after):
        score, slope = work[side]
        peak = jnp.max(top, axis=0, keepdims=True)
        total, delta, top = zero, zero, lowest
        turn(after, 1 - side)
        for n in range(steps):
            top = products(1 - side, n, top)
            part = jnp.exp2(score[span(n)] - peak)
            score[span(n)] = part
            soft[block(n), :, lanes(g)] = part.astype(jnp.bfloat16).reshape(-1, pair_rows, tokens)
            total = total + jnp.sum(part.reshape(-1, 8, tokens), axis=0)
            delta = delta + jnp.sum((part * slope[span(n)]).reshape(-1, 8, tokens), axis=0)
        inverse = 1.0 / jnp.sum(total, axis=0, keepdims=True)
        delta = jnp.sum(delta, axis=0, keepdims=True) * inverse
        inverse = jnp.where(live, inverse, 0.0)
        query_t, upstream_t = turned[side]
        query_s[lanes(g)] = (query_t[...].astype(jnp.float32) * (inverse * scale)).T.astype(jnp.bfloat16)
        upstream_s[lanes(g)] = (upstream_t[...].astype(jnp.float32) * inverse).T.astype(jnp.bfloat16)
        result = query_products(before)
        for n in range(steps):
            part = (score[span(n)] * (slope[span(n)] - delta)).astype(jnp.bfloat16)
            slopes[block(n), :, lanes(g)] = part.reshape(-1, pair_rows, tokens)
        grad_query[:, columns(before)] = (result * factor).T.astype(jnp.bfloat16)
        return top, inverse * scale

    final = groups - 1
    slopes[:, :, final * tokens:] = jnp.zeros((slopes.shape[0], pair_rows, tokens), jnp.bfloat16)
    turn(0, 0)
    top = lowest
    for n in range(steps):
        top = products(0, n, top)

    def two_groups(i, carry):
        top, factor = carry
        g = 2 * i
        top, factor = one_group(g, 0, top, lax.rem(g + final, groups), factor, g + 1)
        return one_group(g + 1, 1, top, g, factor, lax.rem(g + 2, groups))

    top, factor = lax.fori_loop(0, groups // 2, two_groups, (top, jnp.zeros((1, tokens), jnp.float32)))
    grad_query[:, final * HEAD_WIDTH:] = (query_products(final) * factor).T.astype(jnp.bfloat16)


def page_gradients(pair, tokens, soft, slopes, query_s, upstream_s, grads):
    groups = query_s.shape[0] // tokens
    for part, (left, right) in enumerate(((slopes, query_s), (soft, upstream_s))):
        value = 0.0
        for g in range(groups):
            lanes = pl.ds(g * tokens, tokens)
            value = value + jnp.dot(left[pair, :, lanes], right[lanes], preferred_element_type=jnp.float32)
        grads[pair, part] = value.reshape(SLOTS, -1, HEAD_WIDTH)


def whole_kernel(share, page_count, tables_hbm, lengths, query_hbm, upstream_hbm, key_hbm, value_hbm,
                 grad_query_hbm, grad_key, grad_value,
                 tables, key_pool, value_pool, ranks, query, upstream, grad_query, pages, keys_t, query_a, upstream_a,
                 query_b, upstream_b, score_a, slope_a, score_b, slope_b, soft, slopes,
                 query_s, upstream_s, grads, stage, recv, x_out, x_in, z_out, z_in, total, packed, back_stage, back,
                 copy_sem, spread_send, spread_recv, send_sem, recv_sem, x_send, x_recv, z_send, z_recv,
                 back_send, back_recv):
    own, head, own_x, own_z, rings = place()
    x_count = lax.axis_size("resp") // rings
    target, origin = spread_peers(own_x, own_z, head, rings, x_count)
    buddy = (own_x + 1 - 2 * lax.rem(own_x, 2)) * rings + own_z

    def ring(d):
        return own_x * rings + mod(own_z + d, rings)

    neighbours = [buddy] + [ring(d) for d in ((1, -1, 2, -2) if rings > 4 else (1, -1, 2))]
    messages = x_count * rings
    tokens = query.shape[0]
    side = lax.rem(own_x, 2)
    half = rings // 2
    loads = [
        pltpu.make_async_copy(source, place, copy_sem.at[n])
        for n, (source, place) in enumerate(
            ((key_hbm, key_pool), (value_hbm, value_pool), (query_hbm, query), (upstream_hbm, upstream),
             (tables_hbm, tables))
        )
    ]
    for load in loads:
        load.start()
    barrier = pltpu.get_barrier_semaphore()

    def greet(i, carry):
        x, h, z = target(i)
        pl.semaphore_signal(barrier, inc=1, device_id=(x * rings + z, h), device_id_type=MESH)
        x, k, z = origin(i)
        pl.semaphore_signal(barrier, inc=1, device_id=(x * rings + z, k), device_id_type=MESH)
        return carry

    lax.fori_loop(0, messages, greet, 0)
    for peer in neighbours:
        pl.semaphore_signal(barrier, inc=1, device_id=(peer, head), device_id_type=MESH)

    loads[4].wait()
    picked = []
    for prompt in range(x_count // 2):
        picked += local_slots(tables, prompt, own, share, page_count)
    loads[0].wait()
    loads[1].wait()
    for n, slot in enumerate(picked):
        page = jnp.maximum(slot, 0)
        for h in range(rings):
            columns = slice(h * HEAD_WIDTH, (h + 1) * HEAD_WIDTH)
            stage[n, h, :ROWS, :] = key_pool[page, :, columns]
            stage[n, h, ROWS:, :] = value_pool[page, :, columns]
    pl.semaphore_wait(barrier, 2 * messages + len(neighbours))

    def send(i, carry):
        x, h, z = target(i)
        pltpu.make_async_remote_copy(
            src_ref=stage.at[x, h], dst_ref=recv.at[own], send_sem=spread_send, recv_sem=spread_recv,
            device_id=(x * rings + z, h), device_id_type=MESH,
        ).start()
        return carry

    lax.fori_loop(0, messages, send, 0)
    owners = prompt_owners(tables, own_x // 2, share, page_count)
    for device in range(x_count * rings):
        rank = jnp.int32(0)
        for n, owner in enumerate(owners):
            rank = jnp.where(owner == device, n, rank)
        ranks[device] = rank
    pltpu.make_async_copy(recv, recv, spread_recv).wait()

    mine = 2 * own_z + side
    for n, owner in enumerate(owners):
        piece = recv[owner]
        pages[0, mine, n * ROWS:(n + 1) * ROWS, :] = piece[:ROWS]
        pages[1, mine, n * ROWS:(n + 1) * ROWS, :] = piece[ROWS:]

    copies = []
    moving = {}

    def push(name, chunk, part, peer):
        slot = len(moving)
        copy = pltpu.make_async_remote_copy(
            src_ref=pages.at[part, chunk], dst_ref=pages.at[part, chunk],
            send_sem=send_sem.at[slot], recv_sem=recv_sem.at[slot],
            device_id=(peer, head), device_id_type=MESH,
        )
        copy.start()
        copies.append(copy)
        moving[name] = copy

    def relay(d, part):
        way = 1 if d > 0 else -1
        chunk = 2 * mod(own_z - d, rings) + side
        push(("z", d + way, part), chunk, part, ring(way))
        if part == (0 if way > 0 else 1):
            push(("z", half, part), chunk, part, ring(2 * way))

    for part in (0, 1):
        push(("x", part, 0), mine, part, buddy)
    for d in ((2, -2, 1, -1) if half == 4 else (2, 1, -1)):
        for part in (0, 1):
            push(("z", d, part), mine, part, ring(d))
    for d in ((2, -2, 0, 3, -3, 4, 1, -1) if half == 4 else (0, 2, 1, -1)):
        for part in (0, 1):
            if d == 0:
                moving["x", part, 0].wait_recv()
                for near in (1, -1):
                    push(("w", near, part), 2 * own_z + 1 - side, part, ring(near))
                continue
            moving["z", d, part].wait_recv()
            if half == 4 and abs(d) == 2:
                relay(d, part)
            if abs(d) > 1:
                push(("x", part, d), 2 * mod(own_z - d, rings) + side, part, buddy)
    for name, copy in moving.items():
        if name[0] == "w" or name[0] == "x" and name[2] != 0:
            copy.wait_recv()

    loads[2].wait()
    loads[3].wait()
    attention_phase(lengths[0], query, upstream, pages, keys_t, ((score_a, slope_a), (score_b, slope_b)),
                    ((query_a, upstream_a), (query_b, upstream_b)), soft, slopes, query_s, upstream_s, grad_query)
    store_query = pltpu.make_async_copy(grad_query, grad_query_hbm, copy_sem.at[0])
    store_query.start()

    far = [4, 3, -3, 2, -2] if half == 4 else [2]
    x_moving, z_moving = {}, {}

    def x_push(n, d, added):
        for part in (0, 1):
            value = grads[mod(own_z + d, rings), part, 1 - side]
            for term in added:
                value = value + z_arrived(term, part)
            x_out[n, part] = value.astype(jnp.bfloat16)
        copy = pltpu.make_async_remote_copy(
            src_ref=x_out.at[n], dst_ref=x_in.at[n], send_sem=x_send.at[n], recv_sem=x_recv.at[n],
            device_id=(buddy, head), device_id_type=MESH,
        )
        copy.start()
        copies.append(copy)
        x_moving[n] = copy

    def z_arrived(name, part):
        copy, n = z_moving[name, part]
        copy.wait_recv()
        return z_in[n].astype(jnp.float32)

    def z_push(name, part, value, device):
        n = len(z_moving)
        z_out[n] = value.astype(jnp.bfloat16)
        copy = pltpu.make_async_remote_copy(
            src_ref=z_out.at[n], dst_ref=z_in.at[n], send_sem=z_send.at[n], recv_sem=z_recv.at[n],
            device_id=(device, head), device_id_type=MESH,
        )
        copy.start()
        copies.append(copy)
        z_moving[name, part] = (copy, n)

    def far_push(d):
        n = far.index(d)
        way = 1 if d > 0 else -1
        x_moving[n].wait_recv()
        for part in (0, 1):
            value = grads[mod(own_z + d, rings), part, side] + x_in[n, part].astype(jnp.float32)
            if half == 4 and abs(d) == 2:
                value = value + z_arrived(("far", 3 * way), part)
                if part == (0 if way > 0 else 1):
                    value = value + z_arrived(("far", 4), part)
            if abs(d) == 2:
                z_push(("far", d), part, value, ring(d))
            elif abs(d) == 3:
                z_push(("far", d), part, value, ring(way))
            else:
                z_push(("far", d), part, value, ring(2 if part == 0 else -2))

    def near_push(d):
        for flip in (0, 1):
            for part in (0, 1):
                value = grads[mod(own_z + d, rings), part, 1 - side if flip else side]
                z_push(("near", d, flip), part, value, ring(d))

    def compute(d):
        page_gradients(mod(own_z + d, rings), tokens, soft, slopes, query_s, upstream_s, grads)

    for n, d in enumerate(far):
        compute(d)
        x_push(n, d, ())
    early = [d for d in far if abs(d) > 2]
    late = [d for d in far if abs(d) == 2]
    for n, d in enumerate((1, -1, 0)):
        compute(d)
        if d != 0:
            near_push(d)
        if n < len(early):
            far_push(early[n])
    x_push(len(far), 0, (("near", 1, 1), ("near", -1, 1)))
    for d in late:
        far_push(d)
    for part in (0, 1):
        value = grads[own_z, part, side]
        for name in [("near", 1, 0), ("near", -1, 0)] + [("far", d) for d in late]:
            value = value + z_arrived(name, part)
        if part == 0:
            x_moving[len(far)].wait_recv()
        total[part] = value + x_in[len(far), part].astype(jnp.float32)

    for n in range(rings):
        packed[n, :ROWS, :] = total[0, n * ROWS:(n + 1) * ROWS, :].astype(jnp.bfloat16)
        packed[n, ROWS:, :] = total[1, n * ROWS:(n + 1) * ROWS, :].astype(jnp.bfloat16)
    for device in range(x_count * rings):
        back_stage[device] = packed[ranks[device]]

    def send_back(i, carry):
        x, k, z = origin(i)
        pltpu.make_async_remote_copy(
            src_ref=back_stage.at[x * rings + z], dst_ref=back.at[own_x, head],
            send_sem=back_send, recv_sem=back_recv,
            device_id=(x * rings + z, k), device_id_type=MESH,
        ).start()
        return carry

    lax.fori_loop(0, messages, send_back, 0)
    pltpu.make_async_copy(back, back, back_recv).wait()
    for page in range(PAGES_DEV):
        takes = [(slot == page).astype(jnp.float32) for slot in picked]
        for h in range(rings):
            columns = slice(h * HEAD_WIDTH, (h + 1) * HEAD_WIDTH)
            value = jnp.zeros((2 * ROWS, HEAD_WIDTH), jnp.float32)
            for n, take in enumerate(takes):
                value = value + back[n, h].astype(jnp.float32) * take
            grad_key[page, :, columns] = value[:ROWS]
            grad_value[page, :, columns] = value[ROWS:]
    for copy in copies:
        copy.wait_send()
    pltpu.make_async_copy(stage, stage, spread_send).wait()
    pltpu.make_async_copy(back_stage, back_stage, back_send).wait()
    store_query.wait()


def gradients(tables, lengths, query, upstream, key_pool, value_pool):
    rings = lax.axis_size("kvh")
    devices = lax.axis_size("resp")
    x_count = devices // rings
    share = 2 * rings
    page_count = tables.shape[0]
    tokens, width = query.shape
    rows = rings * ROWS
    chunks = SLOTS * rings
    count = chunks * rows
    query_rows = tokens * (width // HEAD_WIDTH)
    z_copies = 2 * rings + 2
    gathers = 4 * rings - 2
    out = jax.ShapeDtypeStruct((PAGES_DEV, ROWS, rings * HEAD_WIDTH), jnp.float32)
    bf16, f32 = jnp.bfloat16, jnp.float32
    vmem = pl.BlockSpec(memory_space=pltpu.VMEM)
    smem = pl.BlockSpec(memory_space=pltpu.SMEM)
    anywhere = pl.BlockSpec(memory_space=pl.ANY)
    dma = pltpu.SemaphoreType.DMA
    return pl.pallas_call(
        functools.partial(whole_kernel, share, page_count),
        out_shape=(jax.ShapeDtypeStruct(query.shape, bf16), out, out),
        in_specs=[anywhere, smem, anywhere, anywhere, anywhere, anywhere],
        out_specs=(anywhere, vmem, vmem),
        scratch_shapes=[
            pltpu.SMEM(tables.shape, jnp.int32),
            pltpu.VMEM(key_pool.shape, bf16),
            pltpu.VMEM(key_pool.shape, bf16),
            pltpu.SMEM((devices,), jnp.int32),
            pltpu.VMEM((tokens, width), bf16),
            pltpu.VMEM((tokens, width), bf16),
            pltpu.VMEM((tokens, width), bf16),
            pltpu.VMEM((2, chunks, rows, HEAD_WIDTH), bf16),
            pltpu.VMEM((HEAD_WIDTH, count), bf16),
            pltpu.VMEM((HEAD_WIDTH, tokens), bf16),
            pltpu.VMEM((HEAD_WIDTH, tokens), bf16),
            pltpu.VMEM((HEAD_WIDTH, tokens), bf16),
            pltpu.VMEM((HEAD_WIDTH, tokens), bf16),
            pltpu.VMEM((count, tokens), f32),
            pltpu.VMEM((count, tokens), f32),
            pltpu.VMEM((count, tokens), f32),
            pltpu.VMEM((count, tokens), f32),
            pltpu.VMEM((rings, 2 * rows, query_rows), bf16),
            pltpu.VMEM((rings, 2 * rows, query_rows), bf16),
            pltpu.VMEM((query_rows, HEAD_WIDTH), bf16),
            pltpu.VMEM((query_rows, HEAD_WIDTH), bf16),
            pltpu.VMEM((rings, 2, SLOTS, rows, HEAD_WIDTH), f32),
            pltpu.VMEM((x_count, rings, 2 * ROWS, HEAD_WIDTH), bf16),
            pltpu.VMEM((devices, 2 * ROWS, HEAD_WIDTH), bf16),
            pltpu.VMEM((rings - 2, 2, rows, HEAD_WIDTH), bf16),
            pltpu.VMEM((rings - 2, 2, rows, HEAD_WIDTH), bf16),
            pltpu.VMEM((z_copies, rows, HEAD_WIDTH), bf16),
            pltpu.VMEM((z_copies, rows, HEAD_WIDTH), bf16),
            pltpu.VMEM((2, rows, HEAD_WIDTH), f32),
            pltpu.VMEM((rings, 2 * ROWS, HEAD_WIDTH), bf16),
            pltpu.VMEM((devices, 2 * ROWS, HEAD_WIDTH), bf16),
            pltpu.VMEM((x_count, rings, 2 * ROWS, HEAD_WIDTH), bf16),
            dma((5,)),
            dma,
            dma,
            dma((gathers,)),
            dma((gathers,)),
            dma((rings - 2,)),
            dma((rings - 2,)),
            dma((z_copies,)),
            dma((z_copies,)),
            dma,
            dma,
        ],
        compiler_params=pltpu.CompilerParams(
            collective_id=0, has_side_effects=True, vmem_limit_bytes=60 * 2**20
        ),
    )(tables, lengths, query, upstream, key_pool, value_pool)


def shards(query, output_gradient, prompt_key_pool, prompt_value_pool, block_tables, lengths):
    grad_query, grad_key, grad_value = gradients(
        block_tables.T, lengths, query[0], output_gradient[0], prompt_key_pool, prompt_value_pool
    )
    return grad_query[None], grad_key, grad_value


def solution(mesh):
    placed = (
        P("resp", None, "kvh"),
        P("resp", None, "kvh"),
        P("resp", "kvh", None),
        P("resp", "kvh", None),
        P(),
        P("resp"),
    )
    return jax.shard_map(
        shards,
        mesh=mesh,
        in_specs=placed,
        out_specs=(P("resp", None, "kvh"), P("resp", "kvh", None), P("resp", "kvh", None)),
        check_vma=False,
    )
```

```python
import functools

import jax
import jax.numpy as jnp
from jax import lax
from jax.experimental import pallas as pl
from jax.experimental.pallas import tpu as pltpu
from jax.sharding import PartitionSpec as P

QUERY_HEADS = 64
KEY_VALUE_HEADS = 8
HEAD_WIDTH = 128
PAGES_DEV = 4
SLOTS = 2
ROWS = 16
MESH = pl.DeviceIdType.MESH
LOG2E = 1.4426950408889634
STEP_ROWS = 512


def place():
    rings = lax.axis_size("kvh")
    own = lax.axis_index("resp")
    head = lax.axis_index("kvh")
    return own, head, own // rings, lax.rem(own, rings), rings


def mod(value, size):
    return lax.rem(value + 2 * size, size)


def local_slots(tables, prompt, own, share, pages):
    first, second, count = jnp.int32(-1), jnp.int32(-1), jnp.int32(0)
    for j in range(pages):
        page = tables[j, prompt * share]
        hit = (page // PAGES_DEV) == own
        local = lax.rem(page, PAGES_DEV)
        first = jnp.where(hit & (count == 0), local, first)
        second = jnp.where(hit & (count == 1), local, second)
        count = count + hit.astype(jnp.int32)
    return first, second


def prompt_owners(tables, prompt, share, pages):
    held = [tables[j, prompt * share] // PAGES_DEV for j in range(pages)]
    ranks = []
    for j in range(pages):
        below = jnp.int32(0)
        for i in range(pages):
            if i != j:
                below = below + (held[i] < held[j]).astype(jnp.int32)
        ranks.append(below // SLOTS)
    owners = []
    for n in range(pages // SLOTS):
        owner = jnp.int32(0)
        for j in range(pages):
            owner = jnp.where(ranks[j] == n, held[j], owner)
        owners.append(owner)
    return owners


def spread_peers(own_x, own_z, head, rings, x_count):
    def around(n, middle, size):
        return mod(middle + (1 - 2 * lax.rem(n, 2)) * ((n + 1) // 2), size)

    def target(i):
        dx, dh = around(lax.rem(i, x_count), x_count // 2, x_count), around(i // x_count, rings // 2 + 1, rings)
        x = lax.rem(own_x + dx, x_count)
        h = lax.rem(head + dh, rings)
        z = mod(own_z - dh + 1, rings)
        return x, h, z

    def origin(i):
        dx, dk = around(lax.rem(i, x_count), x_count // 2, x_count), around(i // x_count, rings // 2 - 1, rings)
        x = lax.rem(own_x + dx, x_count)
        k = lax.rem(head + dk, rings)
        z = mod(own_z - dk - 1, rings)
        return x, k, z

    return target, origin


def attention_phase(length, query, upstream, pages, keys_t, work, turned, soft, slopes, query_s, upstream_s, grad_query):
    tokens, width = query.shape
    groups = width // HEAD_WIDTH
    chunks, rows = pages.shape[1], pages.shape[2]
    count = chunks * rows
    step = min(STEP_ROWS, count)
    steps = count // step
    scale = HEAD_WIDTH ** -0.5
    pair_rows = soft.shape[1]
    for c in range(chunks):
        keys_t[:, c * rows:(c + 1) * rows] = pages[0, c].T

    def columns(g):
        return pl.ds(pl.multiple_of(g * HEAD_WIDTH, HEAD_WIDTH), HEAD_WIDTH)

    def lanes(g):
        return pl.ds(pl.multiple_of(g * tokens, tokens), tokens)

    def span(n):
        return pl.ds(n * step, step)

    def block(n):
        return pl.ds(n * step // pair_rows, step // pair_rows)

    def held(part, n):
        return pages[part, n * step // rows:(n + 1) * step // rows].reshape(step, HEAD_WIDTH)

    lowest = jnp.full((8, tokens), -jnp.inf, jnp.float32)
    zero = jnp.zeros((8, tokens), jnp.float32)
    live = lax.broadcasted_iota(jnp.int32, (1, tokens), 1) < length

    def turn(g, side):
        query_t, upstream_t = turned[side]
        query_t[...] = query[:, columns(g)].T
        upstream_t[...] = upstream[:, columns(g)].T

    def products(side, n, top):
        query_t, upstream_t = turned[side]
        score, slope = work[side]
        part = jnp.dot(held(0, n), query_t[...], preferred_element_type=jnp.float32) * (scale * LOG2E)
        score[span(n)] = part
        slope[span(n)] = jnp.dot(held(1, n), upstream_t[...], preferred_element_type=jnp.float32)
        return jnp.maximum(top, jnp.max(part.reshape(-1, 8, tokens), axis=0))

    def query_products(g):
        block_slopes = slopes[:, :, lanes(g)].reshape(count, tokens)
        return jnp.dot(keys_t[...], block_slopes, preferred_element_type=jnp.float32)

    def one_group(g, side, top, before, factor, after):
        score, slope = work[side]
        peak = jnp.max(top, axis=0, keepdims=True)
        total, delta, top = zero, zero, lowest
        turn(after, 1 - side)
        for n in range(steps):
            top = products(1 - side, n, top)
            part = jnp.exp2(score[span(n)] - peak)
            score[span(n)] = part
            soft[block(n), :, lanes(g)] = part.astype(jnp.bfloat16).reshape(-1, pair_rows, tokens)
            total = total + jnp.sum(part.reshape(-1, 8, tokens), axis=0)
            delta = delta + jnp.sum((part * slope[span(n)]).reshape(-1, 8, tokens), axis=0)
        inverse = 1.0 / jnp.sum(total, axis=0, keepdims=True)
        delta = jnp.sum(delta, axis=0, keepdims=True) * inverse
        inverse = jnp.where(live, inverse, 0.0)
        query_t, upstream_t = turned[side]
        query_s[lanes(g)] = (query_t[...].astype(jnp.float32) * (inverse * scale)).T.astype(jnp.bfloat16)
        upstream_s[lanes(g)] = (upstream_t[...].astype(jnp.float32) * inverse).T.astype(jnp.bfloat16)
        result = query_products(before)
        for n in range(steps):
            part = (score[span(n)] * (slope[span(n)] - delta)).astype(jnp.bfloat16)
            slopes[block(n), :, lanes(g)] = part.reshape(-1, pair_rows, tokens)
        grad_query[:, columns(before)] = (result * factor).T.astype(jnp.bfloat16)
        return top, inverse * scale

    final = groups - 1
    slopes[:, :, final * tokens:] = jnp.zeros((slopes.shape[0], pair_rows, tokens), jnp.bfloat16)
    turn(0, 0)
    top = lowest
    for n in range(steps):
        top = products(0, n, top)

    def two_groups(i, carry):
        top, factor = carry
        g = 2 * i
        top, factor = one_group(g, 0, top, lax.rem(g + final, groups), factor, g + 1)
        return one_group(g + 1, 1, top, g, factor, lax.rem(g + 2, groups))

    top, factor = lax.fori_loop(0, groups // 2, two_groups, (top, jnp.zeros((1, tokens), jnp.float32)))
    grad_query[:, final * HEAD_WIDTH:] = (query_products(final) * factor).T.astype(jnp.bfloat16)


def page_gradients(pair, tokens, soft, slopes, query_s, upstream_s, grads):
    groups = query_s.shape[0] // tokens
    for part, (left, right) in enumerate(((slopes, query_s), (soft, upstream_s))):
        value = 0.0
        for g in range(groups):
            lanes = pl.ds(g * tokens, tokens)
            value = value + jnp.dot(left[pair, :, lanes], right[lanes], preferred_element_type=jnp.float32)
        grads[pair, part] = value.reshape(SLOTS, -1, HEAD_WIDTH)


def whole_kernel(share, page_count, tables_hbm, lengths, query_hbm, upstream_hbm, key_hbm, value_hbm,
                 grad_query_hbm, grad_key, grad_value,
                 tables, key_pool, value_pool, ranks, query, upstream, grad_query, pages, keys_t, query_a, upstream_a,
                 query_b, upstream_b, score_a, slope_a, score_b, slope_b, soft, slopes,
                 query_s, upstream_s, grads, stage, recv, x_out, x_in, z_out, z_in, total, packed, back_stage, back,
                 copy_sem, spread_send, spread_recv, send_sem, recv_sem, x_send, x_recv, z_send, z_recv,
                 back_send, back_recv):
    own, head, own_x, own_z, rings = place()
    x_count = lax.axis_size("resp") // rings
    target, origin = spread_peers(own_x, own_z, head, rings, x_count)
    buddy = (own_x + 1 - 2 * lax.rem(own_x, 2)) * rings + own_z

    def ring(d):
        return own_x * rings + mod(own_z + d, rings)

    neighbours = [buddy] + [ring(d) for d in ((1, -1, 2, -2) if rings > 4 else (1, -1, 2))]
    messages = x_count * rings
    tokens = query.shape[0]
    side = lax.rem(own_x, 2)
    half = rings // 2
    loads = [
        pltpu.make_async_copy(source, place, copy_sem.at[n])
        for n, (source, place) in enumerate(
            ((key_hbm, key_pool), (value_hbm, value_pool), (query_hbm, query), (upstream_hbm, upstream),
             (tables_hbm, tables))
        )
    ]
    for load in loads:
        load.start()
    barrier = pltpu.get_barrier_semaphore()

    def greet(i, carry):
        x, h, z = target(i)
        pl.semaphore_signal(barrier, inc=1, device_id=(x * rings + z, h), device_id_type=MESH)
        x, k, z = origin(i)
        pl.semaphore_signal(barrier, inc=1, device_id=(x * rings + z, k), device_id_type=MESH)
        return carry

    lax.fori_loop(0, messages, greet, 0)
    for peer in neighbours:
        pl.semaphore_signal(barrier, inc=1, device_id=(peer, head), device_id_type=MESH)

    loads[4].wait()
    picked = []
    for prompt in range(x_count // 2):
        picked += local_slots(tables, prompt, own, share, page_count)
    loads[0].wait()
    loads[1].wait()
    for n, slot in enumerate(picked):
        page = jnp.maximum(slot, 0)
        for h in range(rings):
            columns = slice(h * HEAD_WIDTH, (h + 1) * HEAD_WIDTH)
            stage[n, h, :ROWS, :] = key_pool[page, :, columns]
            stage[n, h, ROWS:, :] = value_pool[page, :, columns]
    pl.semaphore_wait(barrier, 2 * messages + len(neighbours))

    def send(i, carry):
        x, h, z = target(i)
        pltpu.make_async_remote_copy(
            src_ref=stage.at[x, h], dst_ref=recv.at[own], send_sem=spread_send, recv_sem=spread_recv,
            device_id=(x * rings + z, h), device_id_type=MESH,
        ).start()
        return carry

    lax.fori_loop(0, messages, send, 0)
    owners = prompt_owners(tables, own_x // 2, share, page_count)
    for device in range(x_count * rings):
        rank = jnp.int32(0)
        for n, owner in enumerate(owners):
            rank = jnp.where(owner == device, n, rank)
        ranks[device] = rank
    pltpu.make_async_copy(recv, recv, spread_recv).wait()

    mine = 2 * own_z + side
    for n, owner in enumerate(owners):
        piece = recv[owner]
        pages[0, mine, n * ROWS:(n + 1) * ROWS, :] = piece[:ROWS]
        pages[1, mine, n * ROWS:(n + 1) * ROWS, :] = piece[ROWS:]

    copies = []
    moving = {}

    def push(name, chunk, part, peer):
        slot = len(moving)
        copy = pltpu.make_async_remote_copy(
            src_ref=pages.at[part, chunk], dst_ref=pages.at[part, chunk],
            send_sem=send_sem.at[slot], recv_sem=recv_sem.at[slot],
            device_id=(peer, head), device_id_type=MESH,
        )
        copy.start()
        copies.append(copy)
        moving[name] = copy

    def relay(d, part):
        way = 1 if d > 0 else -1
        chunk = 2 * mod(own_z - d, rings) + side
        push(("z", d + way, part), chunk, part, ring(way))
        if part == (0 if way > 0 else 1):
            push(("z", half, part), chunk, part, ring(2 * way))

    for part in (0, 1):
        push(("x", part, 0), mine, part, buddy)
    for d in ((2, -2, 1, -1) if half == 4 else (2, 1, -1)):
        for part in (0, 1):
            push(("z", d, part), mine, part, ring(d))
    for d in ((2, -2, 0, 3, -3, 4, 1, -1) if half == 4 else (0, 2, 1, -1)):
        for part in (0, 1):
            if d == 0:
                moving["x", part, 0].wait_recv()
                for near in (1, -1):
                    push(("w", near, part), 2 * own_z + 1 - side, part, ring(near))
                continue
            moving["z", d, part].wait_recv()
            if half == 4 and abs(d) == 2:
                relay(d, part)
            if abs(d) > 1:
                push(("x", part, d), 2 * mod(own_z - d, rings) + side, part, buddy)
    for name, copy in moving.items():
        if name[0] == "w" or name[0] == "x" and name[2] != 0:
            copy.wait_recv()

    loads[2].wait()
    loads[3].wait()
    attention_phase(lengths[0], query, upstream, pages, keys_t, ((score_a, slope_a), (score_b, slope_b)),
                    ((query_a, upstream_a), (query_b, upstream_b)), soft, slopes, query_s, upstream_s, grad_query)
    store_query = pltpu.make_async_copy(grad_query, grad_query_hbm, copy_sem.at[0])
    store_query.start()

    far = [4, 3, -3, 2, -2] if half == 4 else [2]
    x_moving, z_moving = {}, {}

    def x_push(n, d, added):
        for part in (0, 1):
            value = grads[mod(own_z + d, rings), part, 1 - side]
            for term in added:
                value = value + z_arrived(term, part)
            x_out[n, part] = value.astype(jnp.bfloat16)
        copy = pltpu.make_async_remote_copy(
            src_ref=x_out.at[n], dst_ref=x_in.at[n], send_sem=x_send.at[n], recv_sem=x_recv.at[n],
            device_id=(buddy, head), device_id_type=MESH,
        )
        copy.start()
        copies.append(copy)
        x_moving[n] = copy

    def z_arrived(name, part):
        copy, n = z_moving[name, part]
        copy.wait_recv()
        return z_in[n].astype(jnp.float32)

    def z_push(name, part, value, device):
        n = len(z_moving)
        z_out[n] = value.astype(jnp.bfloat16)
        copy = pltpu.make_async_remote_copy(
            src_ref=z_out.at[n], dst_ref=z_in.at[n], send_sem=z_send.at[n], recv_sem=z_recv.at[n],
            device_id=(device, head), device_id_type=MESH,
        )
        copy.start()
        copies.append(copy)
        z_moving[name, part] = (copy, n)

    def far_push(d):
        n = far.index(d)
        way = 1 if d > 0 else -1
        x_moving[n].wait_recv()
        for part in (0, 1):
            value = grads[mod(own_z + d, rings), part, side] + x_in[n, part].astype(jnp.float32)
            if half == 4 and abs(d) == 2:
                value = value + z_arrived(("far", 3 * way), part)
                if part == (0 if way > 0 else 1):
                    value = value + z_arrived(("far", 4), part)
            if abs(d) == 2:
                z_push(("far", d), part, value, ring(d))
            elif abs(d) == 3:
                z_push(("far", d), part, value, ring(way))
            else:
                z_push(("far", d), part, value, ring(2 if part == 0 else -2))

    def near_push(d):
        for flip in (0, 1):
            for part in (0, 1):
                value = grads[mod(own_z + d, rings), part, 1 - side if flip else side]
                z_push(("near", d, flip), part, value, ring(d))

    def compute(d):
        page_gradients(mod(own_z + d, rings), tokens, soft, slopes, query_s, upstream_s, grads)

    for n, d in enumerate(far):
        compute(d)
        x_push(n, d, ())
    early = [d for d in far if abs(d) > 2]
    late = [d for d in far if abs(d) == 2]
    for n, d in enumerate((1, -1, 0)):
        compute(d)
        if d != 0:
            near_push(d)
        if n < len(early):
            far_push(early[n])
    x_push(len(far), 0, (("near", 1, 1), ("near", -1, 1)))
    for d in late:
        far_push(d)
    for part in (0, 1):
        value = grads[own_z, part, side]
        for name in [("near", 1, 0), ("near", -1, 0)] + [("far", d) for d in late]:
            value = value + z_arrived(name, part)
        if part == 0:
            x_moving[len(far)].wait_recv()
        total[part] = value + x_in[len(far), part].astype(jnp.float32)

    for n in range(rings):
        packed[n, :ROWS, :] = total[0, n * ROWS:(n + 1) * ROWS, :].astype(jnp.bfloat16)
        packed[n, ROWS:, :] = total[1, n * ROWS:(n + 1) * ROWS, :].astype(jnp.bfloat16)
    for device in range(x_count * rings):
        back_stage[device] = packed[ranks[device]]

    def send_back(i, carry):
        x, k, z = origin(i)
        pltpu.make_async_remote_copy(
            src_ref=back_stage.at[x * rings + z], dst_ref=back.at[own_x, head],
            send_sem=back_send, recv_sem=back_recv,
            device_id=(x * rings + z, k), device_id_type=MESH,
        ).start()
        return carry

    lax.fori_loop(0, messages, send_back, 0)
    pltpu.make_async_copy(back, back, back_recv).wait()
    for page in range(PAGES_DEV):
        takes = [(slot == page).astype(jnp.float32) for slot in picked]
        for h in range(rings):
            columns = slice(h * HEAD_WIDTH, (h + 1) * HEAD_WIDTH)
            value = jnp.zeros((2 * ROWS, HEAD_WIDTH), jnp.float32)
            for n, take in enumerate(takes):
                value = value + back[n, h].astype(jnp.float32) * take
            grad_key[page, :, columns] = value[:ROWS]
            grad_value[page, :, columns] = value[ROWS:]
    for copy in copies:
        copy.wait_send()
    pltpu.make_async_copy(stage, stage, spread_send).wait()
    pltpu.make_async_copy(back_stage, back_stage, back_send).wait()
    store_query.wait()


def settle_kernel(pieces, count, *refs):
    sources, places, held = refs[:count], refs[count:2 * count], refs[2 * count:3 * count]
    arrive, leave = refs[-2:]
    inward, outward = [], []
    for source, place, local in zip(sources, places, held):
        rows = source.shape[0] // pieces
        for n in range(pieces):
            part = pl.ds(n * rows, rows)
            slot = len(inward)
            inward.append(pltpu.make_async_copy(source.at[part], local.at[part], arrive.at[slot]))
            outward.append(pltpu.make_async_copy(local.at[part], place.at[part], leave.at[slot]))
    for copy in inward:
        copy.start()
    for first, second in zip(inward, outward):
        first.wait()
        second.start()
    for copy in outward:
        copy.wait()


def settled(arrays):
    pieces = 2
    anywhere = pl.BlockSpec(memory_space=pl.ANY)
    copies = pieces * len(arrays)
    return pl.pallas_call(
        functools.partial(settle_kernel, pieces, len(arrays)),
        out_shape=tuple(jax.ShapeDtypeStruct(a.shape, a.dtype) for a in arrays),
        in_specs=[anywhere] * len(arrays),
        out_specs=(anywhere,) * len(arrays),
        scratch_shapes=[pltpu.VMEM(a.shape, a.dtype) for a in arrays]
        + [pltpu.SemaphoreType.DMA((copies,)), pltpu.SemaphoreType.DMA((copies,))],
        compiler_params=pltpu.CompilerParams(vmem_limit_bytes=60 * 2**20),
    )(*arrays)


def gradients(tables, lengths, query, upstream, key_pool, value_pool):
    rings = lax.axis_size("kvh")
    devices = lax.axis_size("resp")
    x_count = devices // rings
    share = 2 * rings
    page_count = tables.shape[0]
    tokens, width = query.shape
    rows = rings * ROWS
    chunks = SLOTS * rings
    count = chunks * rows
    query_rows = tokens * (width // HEAD_WIDTH)
    z_copies = 2 * rings + 2
    gathers = 4 * rings - 2
    out = jax.ShapeDtypeStruct((PAGES_DEV, ROWS, rings * HEAD_WIDTH), jnp.float32)
    bf16, f32 = jnp.bfloat16, jnp.float32
    vmem = pl.BlockSpec(memory_space=pltpu.VMEM)
    smem = pl.BlockSpec(memory_space=pltpu.SMEM)
    anywhere = pl.BlockSpec(memory_space=pl.ANY)
    dma = pltpu.SemaphoreType.DMA
    return pl.pallas_call(
        functools.partial(whole_kernel, share, page_count),
        out_shape=(jax.ShapeDtypeStruct(query.shape, bf16), out, out),
        in_specs=[anywhere, smem, anywhere, anywhere, anywhere, anywhere],
        out_specs=(anywhere, vmem, vmem),
        scratch_shapes=[
            pltpu.SMEM(tables.shape, jnp.int32),
            pltpu.VMEM(key_pool.shape, bf16),
            pltpu.VMEM(key_pool.shape, bf16),
            pltpu.SMEM((devices,), jnp.int32),
            pltpu.VMEM((tokens, width), bf16),
            pltpu.VMEM((tokens, width), bf16),
            pltpu.VMEM((tokens, width), bf16),
            pltpu.VMEM((2, chunks, rows, HEAD_WIDTH), bf16),
            pltpu.VMEM((HEAD_WIDTH, count), bf16),
            pltpu.VMEM((HEAD_WIDTH, tokens), bf16),
            pltpu.VMEM((HEAD_WIDTH, tokens), bf16),
            pltpu.VMEM((HEAD_WIDTH, tokens), bf16),
            pltpu.VMEM((HEAD_WIDTH, tokens), bf16),
            pltpu.VMEM((count, tokens), f32),
            pltpu.VMEM((count, tokens), f32),
            pltpu.VMEM((count, tokens), f32),
            pltpu.VMEM((count, tokens), f32),
            pltpu.VMEM((rings, 2 * rows, query_rows), bf16),
            pltpu.VMEM((rings, 2 * rows, query_rows), bf16),
            pltpu.VMEM((query_rows, HEAD_WIDTH), bf16),
            pltpu.VMEM((query_rows, HEAD_WIDTH), bf16),
            pltpu.VMEM((rings, 2, SLOTS, rows, HEAD_WIDTH), f32),
            pltpu.VMEM((x_count, rings, 2 * ROWS, HEAD_WIDTH), bf16),
            pltpu.VMEM((devices, 2 * ROWS, HEAD_WIDTH), bf16),
            pltpu.VMEM((rings - 2, 2, rows, HEAD_WIDTH), bf16),
            pltpu.VMEM((rings - 2, 2, rows, HEAD_WIDTH), bf16),
            pltpu.VMEM((z_copies, rows, HEAD_WIDTH), bf16),
            pltpu.VMEM((z_copies, rows, HEAD_WIDTH), bf16),
            pltpu.VMEM((2, rows, HEAD_WIDTH), f32),
            pltpu.VMEM((rings, 2 * ROWS, HEAD_WIDTH), bf16),
            pltpu.VMEM((devices, 2 * ROWS, HEAD_WIDTH), bf16),
            pltpu.VMEM((x_count, rings, 2 * ROWS, HEAD_WIDTH), bf16),
            dma((5,)),
            dma,
            dma,
            dma((gathers,)),
            dma((gathers,)),
            dma((rings - 2,)),
            dma((rings - 2,)),
            dma((z_copies,)),
            dma((z_copies,)),
            dma,
            dma,
        ],
        compiler_params=pltpu.CompilerParams(
            collective_id=0, has_side_effects=True, vmem_limit_bytes=60 * 2**20
        ),
    )(tables, lengths, query, upstream, key_pool, value_pool)


def shards(query, output_gradient, prompt_key_pool, prompt_value_pool, block_tables, lengths):
    grad_query, grad_key, grad_value = settled(
        gradients(block_tables.T, lengths, query[0], output_gradient[0], prompt_key_pool, prompt_value_pool)
    )
    return grad_query[None], grad_key, grad_value


def solution(mesh):
    placed = (
        P("resp", None, "kvh"),
        P("resp", None, "kvh"),
        P("resp", "kvh", None),
        P("resp", "kvh", None),
        P(),
        P("resp"),
    )
    return jax.shard_map(
        shards,
        mesh=mesh,
        in_specs=placed,
        out_specs=(P("resp", None, "kvh"), P("resp", "kvh", None), P("resp", "kvh", None)),
        check_vma=False,
    )
```
